512 devices in a mesh: member: 16 (over y, core), space: 32 (over z, x).
Axes of the slice: x: 4, y: 8, z: 8, core: 2. Of those that a mesh axis runs over, the one named last changes fastest.
Arguments:
- prior_sample: float32 [256, 1048576], P('member', 'space'), may hold values from -6 to 6
- measured_point_location: int32 [512, 128], P('space'), may hold values from 0 to 32767
- measured_data: float32 [512, 128], P('space'), may hold values from -12 to 12
- measurement_noise_sigma: float32 [512, 128], P('space'), may hold values from 2 to 64
- measured_slots_used: int32 [32], P('space'), may hold values from 512 to 2048, as said below
Outputs:
- analysis: float32 [256, 1048576], P('member', 'space')
The draws below stay inside these ranges and needn't reach their ends.
Inputs may be any that keep to these rules, and one draw needn't show every extreme that they name: measured_slots_used gives for each space block how many of its first slots are in use; some block uses all 2048 slots. `measured_point_location`: each index is a state point of the observation's own space block.
All inputs are finite; a program needn't handle non-finite values.
Results may differ from the reference program's by a relative error of at most 0.000088.
Values sent between devices are 32-bit elements; how exact they have to be, the bound alone decides.
No kernel may reach another device: no remote copies, remote signals or barrier semaphores. Data moves between devices by JAX's collectives and lax.ppermute only.
A program may use at most 64 MiB of HBM per device.

```python
import math
import jax
import jax.numpy as jnp
from jax import lax

SAMPLE_TOTAL = 256
ROW = 128
POINTS_IN_REGION = 32768
REGION_TOTAL = 32
GRID_POINTS = 1048576
OBS_BLK = 2048
OBS_ROWS = 512


def draw_measured_slots_used(key, part):
    counts = jax.random.randint(key, (REGION_TOTAL,), OBS_BLK // 4, OBS_BLK + 1)
    chosen = jax.random.randint(jax.random.fold_in(key, 7), (), 0, REGION_TOTAL)
    full_block = jnp.arange(REGION_TOTAL) == chosen
    return jnp.where(full_block, OBS_BLK, counts).astype(jnp.int32)


def touch_ends(array, own_key, low, top_value):
    shape = array.shape
    index_at = [jax.random.randint(jax.random.fold_in(own_key, axis), (), 0, shape[axis]) for axis in range(len(shape))]
    array = array.at[tuple(index_at)].set(low)
    longest = shape.index(max(shape))
    index_at[longest] = (index_at[longest] + 1) % shape[longest]
    return array.at[tuple(index_at)].set(top_value)


def block_levels(key, shape, split, least, high):
    def one(position, blocks):
        draws = jax.random.uniform(jax.random.fold_in(jax.random.fold_in(key, 6), position), (blocks,), jnp.float32, least / len(split), high / len(split))
        return jnp.repeat(jnp.exp(draws), shape[position] // blocks).reshape((-1,) + (1,) * (len(shape) - position - 1))

    factor_of = one(*split[0])
    for cut in split[1:]:
        factor_of = factor_of * one(*cut)
    return factor_of


def bell_draw(rng, shape, width, limit, shards=(), kind=jnp.bfloat16):
    entries = jax.random.normal(rng, shape, jnp.float32) * width
    if len(shards) > 0:
        entries = block_levels(rng, shape, shards, -0.22, 0.18) * entries
    return jnp.clip(entries, min=-limit, max=limit).astype(kind)


def setup_inputs(seed: int = 0) -> dict:
    key_list = jax.random.split(jax.random.key(seed), 6)
    prior_sample = bell_draw(key_list[0], (SAMPLE_TOTAL, GRID_POINTS), 1.0, 6.0, ((0, 16), (1, 32)), jnp.float32)
    measured_point_location = touch_ends(jax.random.randint(key_list[1], (OBS_ROWS, ROW), 0, POINTS_IN_REGION), jax.random.fold_in(key_list[1], 1), 0, POINTS_IN_REGION - 1).astype(jnp.int32)
    measured_data = bell_draw(key_list[2], (OBS_ROWS, ROW), 3.0, 12.0, ((0, 32),), jnp.float32)
    measurement_noise_sigma = jnp.clip(jnp.exp(math.log(64.0) - 3.465736 * jax.random.uniform(key_list[3], (OBS_ROWS, ROW), jnp.float32) ** block_levels(key_list[3], (OBS_ROWS, ROW), ((0, 32),), -0.2, 0.2)), 2.0, 64.0)
    measured_slots_used = draw_measured_slots_used(jax.random.fold_in(key_list[5], 71), 0)
    return {"prior_sample": prior_sample, "measured_point_location": measured_point_location, "measured_data": measured_data, "measurement_noise_sigma": measurement_noise_sigma, "measured_slots_used": measured_slots_used}


def lower_inverse(lower_factor):
    size_k = lower_factor.shape[0]
    ident = jnp.eye(size_k, dtype=lower_factor.dtype)
    return lax.linalg.triangular_solve(lower_factor, ident, left_side=True, lower=True)

def reference(prior_sample, measured_point_location, measured_data, measurement_noise_sigma, measured_slots_used):
    exact_arithmetic = lax.Precision.HIGHEST
    sample_total = prior_sample.shape[0]
    region_total = prior_sample.reshape(sample_total, REGION_TOTAL, POINTS_IN_REGION)
    index_blocks = measured_point_location.reshape(REGION_TOTAL, OBS_BLK)
    propagated_grid = jax.vmap(lambda block, places: jnp.take(block, places, axis=1), in_axes=(1, 0), out_axes=1)(region_total, index_blocks)
    propagated_grid = propagated_grid.reshape(sample_total, REGION_TOTAL * OBS_BLK)
    slots = jnp.arange(OBS_BLK, dtype=jnp.int32)
    valid = (slots[None, :] < measured_slots_used[:, None]).reshape(-1)
    weight = jnp.where(valid, 1.0 / measurement_noise_sigma.reshape(-1), jnp.zeros_like(measurement_noise_sigma.reshape(-1)))
    sim_mean = lax.optimization_barrier(jnp.mean(propagated_grid, axis=0))
    perturbed = (propagated_grid - sim_mean[None, :]) * weight[None, :]
    innovation = (measured_data.reshape(-1) - sim_mean) * weight
    gram_all = jnp.dot(perturbed, perturbed.T, precision=exact_arithmetic)
    cross = jnp.dot(perturbed, innovation, precision=exact_arithmetic)
    cov_matrix = gram_all + (sample_total - 1) * jnp.eye(sample_total, dtype=gram_all.dtype)
    lower_factor = jnp.linalg.cholesky(cov_matrix)
    inverse = lower_inverse(lower_factor)
    projected = jnp.dot(inverse, cross, precision=exact_arithmetic)
    mean_weight = jnp.dot(inverse.T, projected, precision=exact_arithmetic)
    weight_matrix_update = math.sqrt(sample_total - 1) * inverse + mean_weight[None, :]
    prior_average = lax.optimization_barrier(jnp.mean(prior_sample, axis=0))
    return prior_average[None, :] + jnp.dot(weight_matrix_update, prior_sample - prior_average[None, :], precision=exact_arithmetic)
```

```python
import math

import jax
import jax.numpy as jnp
from jax import lax
from jax.experimental import pallas as pl
from jax.experimental.pallas import tpu as pltpu
from jax.sharding import PartitionSpec as P

MEMBER = "member"
SPACE = "space"
LANES = 128


def pick_kernel(places_ref, state_ref, out_ref):
    rows = out_ref.shape[0]
    members = state_ref.shape[0]
    lane = lax.broadcasted_iota(jnp.int32, (members, LANES), 1)

    def one_row(row, carry):
        total = jnp.zeros((members, LANES), jnp.float32)
        for slot in range(LANES):
            place = places_ref[row, slot]
            tile = pl.multiple_of((place >> 7) << 7, LANES)
            cells = state_ref[:, pl.ds(tile, LANES)]
            turned = pltpu.roll(cells, (slot - place) & (LANES - 1), 1)
            total = jnp.where(lane == slot, turned, total)
        out_ref[row] = total
        return carry

    lax.fori_loop(0, rows, one_row, 0)


def pick(places, state):
    rows = places.shape[0]
    members = state.shape[0]
    return pl.pallas_call(
        pick_kernel,
        out_shape=jax.ShapeDtypeStruct((rows, members, LANES), jnp.float32),
        in_specs=[
            pl.BlockSpec(memory_space=pltpu.SMEM),
            pl.BlockSpec(memory_space=pltpu.VMEM),
        ],
        out_specs=pl.BlockSpec(memory_space=pltpu.VMEM),
        compiler_params=pltpu.CompilerParams(vmem_limit_bytes=16 * 2**20),
        cost_estimate=pl.CostEstimate(
            flops=0, bytes_accessed=state.size * 4, transcendentals=0
        ),
    )(places, state)


def sent_to_all(array, axis):
    size = lax.axis_size(axis)
    copies = jnp.broadcast_to(array[None], (size, *array.shape))
    return lax.all_to_all(copies, axis, 0, 0, tiled=True)


def summed_everywhere(array):
    parts = lax.axis_size(SPACE)
    height = array.shape[0] // parts
    pieces = array.reshape(parts, height, array.shape[1])
    pieces = jnp.sum(lax.all_to_all(pieces, SPACE, 0, 0, tiled=True), axis=0)
    pieces = jnp.sum(sent_to_all(pieces, MEMBER), axis=0)
    return sent_to_all(pieces, SPACE).reshape(array.shape)


def body(
    prior_sample,
    measured_point_location,
    measured_data,
    measurement_noise_sigma,
    measured_slots_used,
):
    exact = lax.Precision.HIGHEST
    own_members, cells = prior_sample.shape
    groups = lax.axis_size(MEMBER)
    total = own_members * groups
    own_cells = cells // groups
    obs = measured_point_location.size // groups

    picked = pick(measured_point_location, prior_sample)
    evolved = lax.all_to_all(picked, MEMBER, 0, 0, tiled=True).reshape(total, obs)

    rank = lax.axis_index(MEMBER)
    value = lax.dynamic_slice_in_dim(measured_data, rank, 1).reshape(obs)
    sigma = lax.dynamic_slice_in_dim(measurement_noise_sigma, rank, 1).reshape(obs)
    slots = rank * obs + jnp.arange(obs, dtype=jnp.int32)
    weight = jnp.where(slots < measured_slots_used[0], 1.0 / sigma, 0.0)
    sim_mean = jnp.mean(evolved, axis=0)
    perturbed = (evolved - sim_mean[None, :]) * weight[None, :]
    innovation = (value - sim_mean) * weight
    gram = jnp.dot(perturbed, perturbed.T, precision=exact)
    cross = jnp.dot(perturbed, innovation, precision=exact)

    state, gram = lax.optimization_barrier((prior_sample, gram))
    forward = state.reshape(own_members, groups, own_cells).swapaxes(0, 1)
    forward = lax.all_to_all(forward, MEMBER, 0, 0, tiled=True).reshape(total, own_cells)

    half = total // 2
    gram = gram.at[:2, half:].set(cross.reshape(2, half))
    gram = summed_everywhere(gram)
    cross = gram[:2, half:].reshape(total)
    lower = jnp.concatenate([gram[:half, :half], gram[half:, :half].T], axis=1)
    gram = jnp.concatenate([lower, gram[half:]], axis=0)
    cov_matrix = gram + (total - 1) * jnp.eye(total, dtype=jnp.float32)
    lower_factor = jnp.linalg.cholesky(cov_matrix)
    inverse = lax.linalg.triangular_solve(
        lower_factor, jnp.eye(total, dtype=jnp.float32), left_side=True, lower=True
    )
    projected = jnp.dot(inverse, cross, precision=exact)
    mean_weight = jnp.dot(inverse.T, projected, precision=exact)
    transform = math.sqrt(total - 1) * inverse + mean_weight[None, :]

    average = jnp.mean(forward, axis=0)
    updated = average[None, :] + jnp.dot(
        transform, forward - average[None, :], precision=exact
    )
    updated = updated.reshape(groups, own_members, own_cells)
    back = lax.all_to_all(updated, MEMBER, 0, 0, tiled=True)
    return back.swapaxes(0, 1).reshape(own_members, cells)


def solution(mesh):
    in_specs = (P(MEMBER, SPACE), P(SPACE, None), P(SPACE, None), P(SPACE, None), P(SPACE))
    return jax.shard_map(
        body, mesh=mesh, in_specs=in_specs, out_specs=P(MEMBER, SPACE), check_vma=False
    )
```

```python
import functools
import math

import jax
import jax.numpy as jnp
from jax import lax
from jax.experimental import pallas as pl
from jax.experimental.pallas import tpu as pltpu
from jax.sharding import PartitionSpec as P

MEMBER = "member"
SPACE = "space"
LANES = 128
SUBLANES = 8
IN_VMEM = pl.BlockSpec(memory_space=pltpu.VMEM)
IN_SMEM = pl.BlockSpec(memory_space=pltpu.SMEM)
KERNEL = pltpu.CompilerParams(vmem_limit_bytes=16 * 2**20)
SMALL = pl.CostEstimate(flops=1024, bytes_accessed=1024, transcendentals=0)


def product(a, b, along):
    return lax.dot_general(
        a,
        b,
        (((1,), (along,)), ((), ())),
        precision=lax.Precision.HIGHEST,
        preferred_element_type=jnp.float32,
    )


def pick_kernel(places_ref, state_ref, out_ref):
    rows, members = out_ref.shape[:2]
    lane = lax.broadcasted_iota(jnp.int32, (members, LANES), 1)

    def one_row(row, carry):
        total = jnp.zeros((members, LANES), jnp.float32)
        for slot in range(LANES):
            place = places_ref[row, slot]
            tile = pl.multiple_of((place >> 7) << 7, LANES)
            cells = state_ref[:, pl.ds(tile, LANES)]
            turned = pltpu.roll(cells, (slot - place) & (LANES - 1), 1)
            total = jnp.where(lane == slot, turned, total)
        out_ref[row] = total
        return carry

    lax.fori_loop(0, rows, one_row, 0)


def pick(places, state):
    return pl.pallas_call(
        pick_kernel,
        out_shape=jax.ShapeDtypeStruct((places.shape[0], state.shape[0], LANES), jnp.float32),
        in_specs=[IN_SMEM, IN_VMEM],
        out_specs=IN_VMEM,
        compiler_params=KERNEL,
        cost_estimate=SMALL,
    )(places, state)


def gram_kernel(rank_ref, used_ref, evolved_ref, data_ref, sigma_ref, out_ref):
    total, obs = evolved_ref.shape
    half = total // 2
    rank = rank_ref[0]
    value = data_ref[pl.ds(rank, 1), :]
    sigma = sigma_ref[pl.ds(rank, 1), :]
    slots = rank * obs + lax.broadcasted_iota(jnp.int32, (1, obs), 1)
    weight = jnp.where(slots < used_ref[0], 1.0 / sigma, 0.0)
    evolved = evolved_ref[...]
    sim_mean = jnp.sum(evolved, axis=0, keepdims=True) * (1.0 / total)
    perturbed = (evolved - sim_mean) * weight
    innovation = jnp.broadcast_to((value - sim_mean) * weight, (SUBLANES, obs))
    out_ref[...] = product(perturbed, perturbed, 1)
    cross = product(innovation, perturbed, 1)
    out_ref[0:1, half:] = cross[0:1, :half]
    out_ref[1:2, half:] = cross[0:1, half:]


def gram_of(rank, used, evolved, data, sigma):
    total = evolved.shape[0]
    return pl.pallas_call(
        gram_kernel,
        out_shape=jax.ShapeDtypeStruct((total, total), jnp.float32),
        in_specs=[IN_SMEM, IN_SMEM, IN_VMEM, IN_VMEM, IN_VMEM],
        out_specs=IN_VMEM,
        compiler_params=KERNEL,
        cost_estimate=SMALL,
    )(rank.reshape(1), used, evolved, data, sigma)


def all_lanes(a, lane):
    return jnp.broadcast_to(a[:, lane : lane + 1], a.shape)


def all_rows(a, row):
    return jnp.broadcast_to(a[row : row + 1, :], a.shape)


def inverse_factor(block):
    size, step = block.shape[0], SUBLANES
    groups = size // step
    row = lax.broadcasted_iota(jnp.int32, (step, size), 0)
    lane = lax.broadcasted_iota(jnp.int32, (step, size), 1)
    left = [block[step * g : step * (g + 1)] for g in range(groups)]
    right = [jnp.where(lane == row + step * g, 1.0, 0.0) for g in range(groups)]
    for p in range(groups):
        left_row = [all_rows(left[p], k) for k in range(step)]
        right_row = [all_rows(right[p], k) for k in range(step)]
        column = [all_lanes(left[p], step * p + j) for j in range(step)]
        a = {(i, j): all_rows(column[j], i) for i in range(step) for j in range(i + 1)}
        factor, scale = {}, []
        for k in range(step):
            scale.append(lax.rsqrt(a[k, k]))
            left_row[k] = left_row[k] * scale[k]
            right_row[k] = right_row[k] * scale[k]
            for i in range(k + 1, step):
                factor[i, k] = a[i, k] * scale[k]
            for i in range(k + 1, step):
                for j in range(k + 1, i + 1):
                    a[i, j] = a[i, j] - factor[i, k] * factor[j, k]
                left_row[i] = left_row[i] - factor[i, k] * left_row[k]
                right_row[i] = right_row[i] - factor[i, k] * right_row[k]
        right[p] = right_row[0]
        for k in range(1, step):
            right[p] = jnp.where(row == k, right_row[k], right[p])
        for g in range(p + 1, groups):
            below = [all_lanes(left[g], step * p + j) for j in range(step)]
            for k in range(step):
                for j in range(k):
                    below[k] = below[k] - below[j] * factor[k, j]
                below[k] = below[k] * scale[k]
            for k in range(step):
                left[g] = left[g] - below[k] * left_row[k]
                right[g] = right[g] - below[k] * right_row[k]
    return jnp.concatenate(right, axis=0)


def transform_kernel(gram_ref, out_ref):
    total = gram_ref.shape[0]
    half = total // 2
    row = lax.broadcasted_iota(jnp.int32, (half, half), 0)
    lane = lax.broadcasted_iota(jnp.int32, (half, half), 1)
    diagonal = jnp.where(row == lane, jnp.float32(total - 1), 0.0)
    first = inverse_factor(gram_ref[:half, :half] + diagonal)
    low = product(gram_ref[half:, :half], first, 1)
    last = inverse_factor(gram_ref[half:, half:] + diagonal - product(low, low, 1))
    corner = -product(last, product(low, first, 0), 0)
    cross_0 = jnp.broadcast_to(gram_ref[0:1, half:], (SUBLANES, half))
    cross_1 = jnp.broadcast_to(gram_ref[1:2, half:], (SUBLANES, half))
    projected_0 = product(cross_0, first, 1)
    projected_1 = product(cross_0, corner, 1) + product(cross_1, last, 1)
    mean_0 = (product(projected_0, first, 0) + product(projected_1, corner, 0))[0:1]
    mean_1 = product(projected_1, last, 0)[0:1]
    spread = math.sqrt(total - 1)
    out_ref[:half, :half] = spread * first + mean_0
    out_ref[:half, half:] = jnp.broadcast_to(mean_1, (half, half))
    out_ref[half:, :half] = spread * corner + mean_0
    out_ref[half:, half:] = spread * last + mean_1


def transform_of(gram):
    return pl.pallas_call(
        transform_kernel,
        out_shape=jax.ShapeDtypeStruct(gram.shape, jnp.float32),
        in_specs=[IN_VMEM],
        out_specs=IN_VMEM,
        compiler_params=KERNEL,
        cost_estimate=SMALL,
    )(gram)


def sent_to_all(array, axis):
    size = lax.axis_size(axis)
    copies = jnp.broadcast_to(array[None], (size, *array.shape))
    return lax.all_to_all(copies, axis, 0, 0, tiled=True)


def summed_everywhere(array):
    parts = lax.axis_size(SPACE)
    height = array.shape[0] // parts
    pieces = array.reshape(parts, height, array.shape[1])
    pieces = jnp.sum(lax.all_to_all(pieces, SPACE, 0, 0, tiled=True), axis=0)
    pieces = jnp.sum(sent_to_all(pieces, MEMBER), axis=0)
    return sent_to_all(pieces, SPACE).reshape(array.shape)


def body(
    prior_sample,
    measured_point_location,
    measured_data,
    measurement_noise_sigma,
    measured_slots_used,
):
    own_members, cells = prior_sample.shape
    groups = lax.axis_size(MEMBER)
    total = own_members * groups
    own_cells = cells // groups

    picked = pick(measured_point_location, prior_sample)
    state, picked = lax.optimization_barrier((prior_sample, picked))
    evolved = lax.all_to_all(picked, MEMBER, 0, 0, tiled=True).reshape(total, LANES)
    forward = state.reshape(own_members, groups, own_cells).swapaxes(0, 1)
    forward = lax.all_to_all(forward, MEMBER, 0, 0, tiled=True).reshape(total, own_cells)

    gram = gram_of(
        lax.axis_index(MEMBER).astype(jnp.int32),
        measured_slots_used,
        evolved,
        measured_data,
        measurement_noise_sigma,
    )
    transform = transform_of(summed_everywhere(gram))

    average = jnp.mean(forward, axis=0)
    updated = average[None, :] + product(transform, forward - average[None, :], 0)
    updated = updated.reshape(groups, own_members, own_cells)
    back = lax.all_to_all(updated, MEMBER, 0, 0, tiled=True)
    return back.swapaxes(0, 1).reshape(own_members, cells)


def solution(mesh):
    in_specs = (P(MEMBER, SPACE), P(SPACE, None), P(SPACE, None), P(SPACE, None), P(SPACE))
    return jax.shard_map(
        body, mesh=mesh, in_specs=in_specs, out_specs=P(MEMBER, SPACE), check_vma=False
    )
```

```python
import functools
import math

import jax
import jax.numpy as jnp
from jax import lax
from jax.experimental import pallas as pl
from jax.experimental.pallas import tpu as pltpu
from jax.sharding import PartitionSpec as P

MEMBER = "member"
SPACE = "space"
LANES = 128
SUBLANES = 8
EARLY = (3, 5, 1, 7)
IN_VMEM = pl.BlockSpec(memory_space=pltpu.VMEM)
IN_SMEM = pl.BlockSpec(memory_space=pltpu.SMEM)
KERNEL = pltpu.CompilerParams(vmem_limit_bytes=16 * 2**20)
SMALL = pl.CostEstimate(flops=1024, bytes_accessed=1024, transcendentals=0)


def product(a, b, along):
    return lax.dot_general(
        a,
        b,
        (((1,), (along,)), ((), ())),
        precision=lax.Precision.HIGHEST,
        preferred_element_type=jnp.float32,
    )


def pick_kernel(places_ref, state_ref, out_ref):
    rows, members = out_ref.shape[:2]
    lane = lax.broadcasted_iota(jnp.int32, (members, LANES), 1)

    def one_row(row, carry):
        total = jnp.zeros((members, LANES), jnp.float32)
        for slot in range(LANES):
            place = places_ref[row, slot]
            tile = pl.multiple_of((place >> 7) << 7, LANES)
            cells = state_ref[:, pl.ds(tile, LANES)]
            turned = pltpu.roll(cells, (slot - place) & (LANES - 1), 1)
            total = jnp.where(lane == slot, turned, total)
        out_ref[row] = total
        return carry

    lax.fori_loop(0, rows, one_row, 0)


def pick(places, state):
    return pl.pallas_call(
        pick_kernel,
        out_shape=jax.ShapeDtypeStruct((places.shape[0], state.shape[0], LANES), jnp.float32),
        in_specs=[IN_SMEM, IN_VMEM],
        out_specs=IN_VMEM,
        compiler_params=KERNEL,
        cost_estimate=SMALL,
    )(places, state)


def gram_kernel(rank_ref, used_ref, evolved_ref, data_ref, sigma_ref, out_ref):
    total, obs = evolved_ref.shape
    half = total // 2
    rank = rank_ref[0]
    value = data_ref[pl.ds(rank, 1), :]
    sigma = sigma_ref[pl.ds(rank, 1), :]
    slots = rank * obs + lax.broadcasted_iota(jnp.int32, (1, obs), 1)
    weight = jnp.where(slots < used_ref[0], 1.0 / sigma, 0.0)
    evolved = evolved_ref[...]
    sim_mean = jnp.sum(evolved, axis=0, keepdims=True) * (1.0 / total)
    perturbed = (evolved - sim_mean) * weight
    innovation = jnp.broadcast_to((value - sim_mean) * weight, (SUBLANES, obs))
    out_ref[...] = product(perturbed, perturbed, 1)
    cross = product(innovation, perturbed, 1)
    out_ref[0:1, half:] = cross[0:1, :half]
    out_ref[1:2, half:] = cross[0:1, half:]


def gram_of(rank, used, evolved, data, sigma):
    total = evolved.shape[0]
    return pl.pallas_call(
        gram_kernel,
        out_shape=jax.ShapeDtypeStruct((total, total), jnp.float32),
        in_specs=[IN_SMEM, IN_SMEM, IN_VMEM, IN_VMEM, IN_VMEM],
        out_specs=IN_VMEM,
        compiler_params=KERNEL,
        cost_estimate=SMALL,
    )(rank.reshape(1), used, evolved, data, sigma)


def all_lanes(a, lane):
    return jnp.broadcast_to(a[:, lane : lane + 1], a.shape)


def all_rows(a, row):
    return jnp.broadcast_to(a[row : row + 1, :], a.shape)


def inverse_factor(block):
    size, step = block.shape[0], SUBLANES
    groups = size // step
    row = lax.broadcasted_iota(jnp.int32, (step, size), 0)
    lane = lax.broadcasted_iota(jnp.int32, (step, size), 1)
    left = [block[step * g : step * (g + 1)] for g in range(groups)]
    right = [jnp.where(lane == row + step * g, 1.0, 0.0) for g in range(groups)]
    for p in range(groups):
        left_row = [all_rows(left[p], k) for k in range(step)]
        right_row = [all_rows(right[p], k) for k in range(step)]
        column = [all_lanes(left[p], step * p + j) for j in range(step)]
        a = {(i, j): all_rows(column[j], i) for i in range(step) for j in range(i + 1)}
        factor, scale = {}, []
        for k in range(step):
            scale.append(lax.rsqrt(a[k, k]))
            left_row[k] = left_row[k] * scale[k]
            right_row[k] = right_row[k] * scale[k]
            for i in range(k + 1, step):
                factor[i, k] = a[i, k] * scale[k]
            for i in range(k + 1, step):
                for j in range(k + 1, i + 1):
                    a[i, j] = a[i, j] - factor[i, k] * factor[j, k]
                left_row[i] = left_row[i] - factor[i, k] * left_row[k]
                right_row[i] = right_row[i] - factor[i, k] * right_row[k]
        right[p] = right_row[0]
        for k in range(1, step):
            right[p] = jnp.where(row == k, right_row[k], right[p])
        for g in range(p + 1, groups):
            below = [all_lanes(left[g], step * p + j) for j in range(step)]
            for k in range(step):
                for j in range(k):
                    below[k] = below[k] - below[j] * factor[k, j]
                below[k] = below[k] * scale[k]
            for k in range(step):
                left[g] = left[g] - below[k] * left_row[k]
                right[g] = right[g] - below[k] * right_row[k]
    return jnp.concatenate(right, axis=0)


def transform_kernel(gram_ref, out_ref):
    total = gram_ref.shape[0]
    half = total // 2
    row = lax.broadcasted_iota(jnp.int32, (half, half), 0)
    lane = lax.broadcasted_iota(jnp.int32, (half, half), 1)
    diagonal = jnp.where(row == lane, jnp.float32(total - 1), 0.0)
    first = inverse_factor(gram_ref[:half, :half] + diagonal)
    low = product(gram_ref[half:, :half], first, 1)
    last = inverse_factor(gram_ref[half:, half:] + diagonal - product(low, low, 1))
    corner = -product(last, product(low, first, 0), 0)
    cross_0 = jnp.broadcast_to(gram_ref[0:1, half:], (SUBLANES, half))
    cross_1 = jnp.broadcast_to(gram_ref[1:2, half:], (SUBLANES, half))
    projected_0 = product(cross_0, first, 1)
    projected_1 = product(cross_0, corner, 1) + product(cross_1, last, 1)
    mean_0 = (product(projected_0, first, 0) + product(projected_1, corner, 0))[0:1]
    mean_1 = product(projected_1, last, 0)[0:1]
    spread = math.sqrt(total - 1)
    out_ref[:half, :half] = spread * first + mean_0
    out_ref[:half, half:] = jnp.broadcast_to(mean_1, (half, half))
    out_ref[half:, :half] = spread * corner + mean_0
    out_ref[half:, half:] = spread * last + mean_1


def transform_of(gram):
    return pl.pallas_call(
        transform_kernel,
        out_shape=jax.ShapeDtypeStruct(gram.shape, jnp.float32),
        in_specs=[IN_VMEM],
        out_specs=IN_VMEM,
        compiler_params=KERNEL,
        cost_estimate=SMALL,
    )(gram)


def apply_kernel(chip_ref, transform_ref, *refs):
    *parts, out_ref, state_ref = refs
    chips = len(parts)
    height = parts[0].shape[0]
    for k, part in enumerate(parts):
        chip = lax.rem(chip_ref[0] - k + chips, chips)
        state_ref[pl.ds(pl.multiple_of(chip * height, height), height), :] = part[...]
    state = state_ref[...]
    average = jnp.sum(state, axis=0, keepdims=True) * (1.0 / state.shape[0])
    out_ref[...] = average + product(transform_ref[...], state - average, 0)


def applied(chip, transform, parts):
    total = transform.shape[0]
    shape = (total, parts[0].shape[1])
    return pl.pallas_call(
        apply_kernel,
        out_shape=jax.ShapeDtypeStruct(shape, jnp.float32),
        in_specs=[IN_SMEM] + [IN_VMEM] * (1 + len(parts)),
        out_specs=IN_VMEM,
        scratch_shapes=[pltpu.VMEM(shape, jnp.float32)],
        compiler_params=pltpu.CompilerParams(vmem_limit_bytes=32 * 2**20),
        cost_estimate=SMALL,
    )(chip.reshape(1), transform, *parts)


def sent_to_all(array, axis):
    size = lax.axis_size(axis)
    copies = jnp.broadcast_to(array[None], (size, *array.shape))
    return lax.all_to_all(copies, axis, 0, 0, tiled=True)


def swapped(array):
    groups = lax.axis_size(MEMBER)
    return lax.ppermute(array, MEMBER, [(i, i ^ 1) for i in range(groups)])


def shifted(array, k):
    if k == 0:
        return array
    groups = lax.axis_size(MEMBER)
    return lax.ppermute(array, MEMBER, [(i, (i + 2 * k) % groups) for i in range(groups)])


def split_kernel(core_ref, state_ref, kept_ref, sent_ref):
    chips, _, width = kept_ref.shape
    core = core_ref[0]
    for chip in range(chips):
        own = pl.multiple_of((2 * chip + core) * width, LANES)
        away = pl.multiple_of((2 * chip + 1 - core) * width, LANES)
        kept_ref[chip] = state_ref[:, pl.ds(own, width)]
        sent_ref[chip] = state_ref[:, pl.ds(away, width)]


def split(core, state, chips):
    members, cells = state.shape
    half = jax.ShapeDtypeStruct((chips, members, cells // chips // 2), jnp.float32)
    return pl.pallas_call(
        split_kernel,
        out_shape=(half, half),
        in_specs=[IN_SMEM, IN_VMEM],
        out_specs=(IN_VMEM, IN_VMEM),
        compiler_params=KERNEL,
        cost_estimate=SMALL,
    )(core.reshape(1), state)


def join_kernel(chip_ref, core_ref, kept_ref, other_ref, *out_refs):
    chips, members, _ = kept_ref.shape
    core = core_ref[0]
    own = pl.ds(pl.multiple_of(core * members, members), members)
    away = pl.ds(pl.multiple_of((1 - core) * members, members), members)
    for k, out_ref in enumerate(out_refs):
        target = lax.rem(chip_ref[0] + k, chips)
        out_ref[own, :] = kept_ref[target]
        out_ref[away, :] = other_ref[target]


def join(chip, core, kept, other):
    chips, members, width = kept.shape
    pair = jax.ShapeDtypeStruct((2 * members, width), jnp.float32)
    return pl.pallas_call(
        join_kernel,
        out_shape=(pair,) * chips,
        in_specs=[IN_SMEM, IN_SMEM, IN_VMEM, IN_VMEM],
        out_specs=(IN_VMEM,) * chips,
        compiler_params=KERNEL,
        cost_estimate=SMALL,
    )(chip.reshape(1), core.reshape(1), kept, other)


def body(
    prior_sample,
    measured_point_location,
    measured_data,
    measurement_noise_sigma,
    measured_slots_used,
):
    own_members, cells = prior_sample.shape
    groups = lax.axis_size(MEMBER)
    chips = groups // 2
    total = own_members * groups
    own_cells = cells // groups
    rank = lax.axis_index(MEMBER).astype(jnp.int32)
    chip, core = rank // 2, lax.rem(rank, 2)

    picked = pick(measured_point_location, prior_sample)
    state, picked = lax.optimization_barrier((prior_sample, picked))
    evolved = lax.all_to_all(picked, MEMBER, 0, 0, tiled=True).reshape(total, LANES)

    kept, sent = split(core, state, chips)
    pairs = join(chip, core, kept, swapped(sent))
    evolved, pairs = lax.optimization_barrier((evolved, pairs))

    gram = gram_of(
        rank, measured_slots_used, evolved, measured_data, measurement_noise_sigma
    )
    parts = {k: shifted(pairs[k], k) for k in EARLY}
    spaces = lax.axis_size(SPACE)
    pieces = gram.reshape(spaces, total // spaces, total)
    pieces = jnp.sum(lax.all_to_all(pieces, SPACE, 0, 0, tiled=True), axis=0)
    pieces, parts = lax.optimization_barrier((pieces, parts))
    pieces = jnp.sum(sent_to_all(pieces, MEMBER), axis=0)
    pieces, pairs = lax.optimization_barrier((pieces, pairs))
    gram = sent_to_all(pieces, SPACE).reshape(total, total)
    for k in range(chips):
        if k not in parts:
            parts[k] = shifted(pairs[k], k)
    transform = transform_of(gram)

    updated = applied(chip, transform, [parts[k] for k in range(chips)])
    updated = updated.reshape(groups, own_members, own_cells)
    back = lax.all_to_all(updated, MEMBER, 0, 0, tiled=True)
    return back.swapaxes(0, 1).reshape(own_members, cells)


def solution(mesh):
    in_specs = (P(MEMBER, SPACE), P(SPACE, None), P(SPACE, None), P(SPACE, None), P(SPACE))
    return jax.shard_map(
        body, mesh=mesh, in_specs=in_specs, out_specs=P(MEMBER, SPACE), check_vma=False
    )
```

```python
import functools
import math

import jax
import jax.numpy as jnp
from jax import lax
from jax.experimental import pallas as pl
from jax.experimental.pallas import tpu as pltpu
from jax.sharding import PartitionSpec as P

MEMBER = "member"
SPACE = "space"
LANES = 128
SUBLANES = 8
FIRST = (3, 5, 2, 6)
THEN = (4, 1, 7, 0)
IN_VMEM = pl.BlockSpec(memory_space=pltpu.VMEM)
IN_SMEM = pl.BlockSpec(memory_space=pltpu.SMEM)
KERNEL = pltpu.CompilerParams(vmem_limit_bytes=16 * 2**20)
SMALL = pl.CostEstimate(flops=1024, bytes_accessed=1024, transcendentals=0)


def product(a, b, along):
    return lax.dot_general(
        a,
        b,
        (((1,), (along,)), ((), ())),
        precision=lax.Precision.HIGHEST,
        preferred_element_type=jnp.float32,
    )


def pick_kernel(places_ref, state_ref, out_ref):
    rows, members = out_ref.shape[:2]
    lane = lax.broadcasted_iota(jnp.int32, (members, LANES), 1)

    def one_row(row, carry):
        total = jnp.zeros((members, LANES), jnp.float32)
        for slot in range(LANES):
            place = places_ref[row, slot]
            tile = pl.multiple_of((place >> 7) << 7, LANES)
            cells = state_ref[:, pl.ds(tile, LANES)]
            turned = pltpu.roll(cells, (slot - place) & (LANES - 1), 1)
            total = jnp.where(lane == slot, turned, total)
        out_ref[row] = total
        return carry

    lax.fori_loop(0, rows, one_row, 0)


def pick(places, state):
    return pl.pallas_call(
        pick_kernel,
        out_shape=jax.ShapeDtypeStruct((places.shape[0], state.shape[0], LANES), jnp.float32),
        in_specs=[IN_SMEM, IN_VMEM],
        out_specs=IN_VMEM,
        compiler_params=KERNEL,
        cost_estimate=SMALL,
    )(places, state)


def gram_kernel(rank_ref, used_ref, evolved_ref, data_ref, sigma_ref, out_ref):
    total, obs = evolved_ref.shape
    half = total // 2
    rank = rank_ref[0]
    value = data_ref[pl.ds(rank, 1), :]
    sigma = sigma_ref[pl.ds(rank, 1), :]
    slots = rank * obs + lax.broadcasted_iota(jnp.int32, (1, obs), 1)
    weight = jnp.where(slots < used_ref[0], 1.0 / sigma, 0.0)
    evolved = evolved_ref[...]
    sim_mean = jnp.sum(evolved, axis=0, keepdims=True) * (1.0 / total)
    perturbed = (evolved - sim_mean) * weight
    innovation = jnp.broadcast_to((value - sim_mean) * weight, (SUBLANES, obs))
    out_ref[...] = product(perturbed, perturbed, 1)
    cross = product(innovation, perturbed, 1)
    out_ref[0:1, half:] = cross[0:1, :half]
    out_ref[1:2, half:] = cross[0:1, half:]


def gram_of(rank, used, evolved, data, sigma):
    total = evolved.shape[0]
    return pl.pallas_call(
        gram_kernel,
        out_shape=jax.ShapeDtypeStruct((total, total), jnp.float32),
        in_specs=[IN_SMEM, IN_SMEM, IN_VMEM, IN_VMEM, IN_VMEM],
        out_specs=IN_VMEM,
        compiler_params=KERNEL,
        cost_estimate=SMALL,
    )(rank.reshape(1), used, evolved, data, sigma)


def all_lanes(a, lane):
    return jnp.broadcast_to(a[:, lane : lane + 1], a.shape)


def all_rows(a, row):
    return jnp.broadcast_to(a[row : row + 1, :], a.shape)


def inverse_factor(block):
    size, step = block.shape[0], SUBLANES
    groups = size // step
    row = lax.broadcasted_iota(jnp.int32, (step, size), 0)
    lane = lax.broadcasted_iota(jnp.int32, (step, size), 1)
    left = [block[step * g : step * (g + 1)] for g in range(groups)]
    right = [jnp.where(lane == row + step * g, 1.0, 0.0) for g in range(groups)]
    for p in range(groups):
        left_row = [all_rows(left[p], k) for k in range(step)]
        right_row = [all_rows(right[p], k) for k in range(step)]
        column = [all_lanes(left[p], step * p + j) for j in range(step)]
        a = {(i, j): all_rows(column[j], i) for i in range(step) for j in range(i + 1)}
        factor, scale = {}, []
        for k in range(step):
            scale.append(lax.rsqrt(a[k, k]))
            left_row[k] = left_row[k] * scale[k]
            right_row[k] = right_row[k] * scale[k]
            for i in range(k + 1, step):
                factor[i, k] = a[i, k] * scale[k]
            for i in range(k + 1, step):
                for j in range(k + 1, i + 1):
                    a[i, j] = a[i, j] - factor[i, k] * factor[j, k]
                left_row[i] = left_row[i] - factor[i, k] * left_row[k]
                right_row[i] = right_row[i] - factor[i, k] * right_row[k]
        right[p] = right_row[0]
        for k in range(1, step):
            right[p] = jnp.where(row == k, right_row[k], right[p])
        for g in range(p + 1, groups):
            below = [all_lanes(left[g], step * p + j) for j in range(step)]
            for k in range(step):
                for j in range(k):
                    below[k] = below[k] - below[j] * factor[k, j]
                below[k] = below[k] * scale[k]
            for k in range(step):
                left[g] = left[g] - below[k] * left_row[k]
                right[g] = right[g] - below[k] * right_row[k]
    return jnp.concatenate(right, axis=0)


def transform_kernel(gram_ref, out_ref):
    total = gram_ref.shape[0]
    half = total // 2
    row = lax.broadcasted_iota(jnp.int32, (half, half), 0)
    lane = lax.broadcasted_iota(jnp.int32, (half, half), 1)
    diagonal = jnp.where(row == lane, jnp.float32(total - 1), 0.0)
    first = inverse_factor(gram_ref[:half, :half] + diagonal)
    low = product(gram_ref[half:, :half], first, 1)
    last = inverse_factor(gram_ref[half:, half:] + diagonal - product(low, low, 1))
    corner = -product(last, product(low, first, 0), 0)
    cross_0 = jnp.broadcast_to(gram_ref[0:1, half:], (SUBLANES, half))
    cross_1 = jnp.broadcast_to(gram_ref[1:2, half:], (SUBLANES, half))
    projected_0 = product(cross_0, first, 1)
    projected_1 = product(cross_0, corner, 1) + product(cross_1, last, 1)
    mean_0 = (product(projected_0, first, 0) + product(projected_1, corner, 0))[0:1]
    mean_1 = product(projected_1, last, 0)[0:1]
    spread = math.sqrt(total - 1)
    out_ref[:half, :half] = spread * first + mean_0
    out_ref[:half, half:] = jnp.broadcast_to(mean_1, (half, half))
    out_ref[half:, :half] = spread * corner + mean_0
    out_ref[half:, half:] = spread * last + mean_1


def transform_of(gram):
    return pl.pallas_call(
        transform_kernel,
        out_shape=jax.ShapeDtypeStruct(gram.shape, jnp.float32),
        in_specs=[IN_VMEM],
        out_specs=IN_VMEM,
        compiler_params=KERNEL,
        cost_estimate=SMALL,
    )(gram)


def apply_kernel(chip_ref, transform_ref, *refs):
    *parts, out_ref, state_ref = refs
    chips = len(parts)
    height = parts[0].shape[0]
    for k, part in zip(FIRST + THEN, parts):
        chip = lax.rem(chip_ref[0] - k + chips, chips)
        state_ref[pl.ds(pl.multiple_of(chip * height, height), height), :] = part[...]
    state = state_ref[...]
    average = jnp.sum(state, axis=0, keepdims=True) * (1.0 / state.shape[0])
    out_ref[...] = average + product(transform_ref[...], state - average, 0)


def applied(chip, transform, parts):
    total = transform.shape[0]
    shape = (total, parts[0].shape[1])
    return pl.pallas_call(
        apply_kernel,
        out_shape=jax.ShapeDtypeStruct(shape, jnp.float32),
        in_specs=[IN_SMEM] + [IN_VMEM] * (1 + len(parts)),
        out_specs=IN_VMEM,
        scratch_shapes=[pltpu.VMEM(shape, jnp.float32)],
        compiler_params=pltpu.CompilerParams(vmem_limit_bytes=32 * 2**20),
        cost_estimate=SMALL,
    )(chip.reshape(1), transform, *parts)


def sent_to_all(array, axis):
    size = lax.axis_size(axis)
    copies = jnp.broadcast_to(array[None], (size, *array.shape))
    return lax.all_to_all(copies, axis, 0, 0, tiled=True)


def swapped(array):
    groups = lax.axis_size(MEMBER)
    return lax.ppermute(array, MEMBER, [(i, i ^ 1) for i in range(groups)])


def shifted(array, k):
    if k == 0:
        return array
    groups = lax.axis_size(MEMBER)
    return lax.ppermute(array, MEMBER, [(i, (i + 2 * k) % groups) for i in range(groups)])


def split_kernel(core_ref, state_ref, kept_ref, sent_ref):
    chips, _, width = kept_ref.shape
    core = core_ref[0]
    for chip in range(chips):
        own = pl.multiple_of((2 * chip + core) * width, LANES)
        away = pl.multiple_of((2 * chip + 1 - core) * width, LANES)
        kept_ref[chip] = state_ref[:, pl.ds(own, width)]
        sent_ref[chip] = state_ref[:, pl.ds(away, width)]


def split(core, state, chips):
    members, cells = state.shape
    half = jax.ShapeDtypeStruct((chips, members, cells // chips // 2), jnp.float32)
    return pl.pallas_call(
        split_kernel,
        out_shape=(half, half),
        in_specs=[IN_SMEM, IN_VMEM],
        out_specs=(IN_VMEM, IN_VMEM),
        compiler_params=KERNEL,
        cost_estimate=SMALL,
    )(core.reshape(1), state)


def join_kernel(chip_ref, core_ref, kept_ref, other_ref, *out_refs):
    chips, members, _ = kept_ref.shape
    core = core_ref[0]
    own = pl.ds(pl.multiple_of(core * members, members), members)
    away = pl.ds(pl.multiple_of((1 - core) * members, members), members)
    for k, out_ref in enumerate(out_refs):
        target = lax.rem(chip_ref[0] + k, chips)
        out_ref[own, :] = kept_ref[target]
        out_ref[away, :] = other_ref[target]


def join(chip, core, kept, other):
    chips, members, width = kept.shape
    pair = jax.ShapeDtypeStruct((2 * members, width), jnp.float32)
    return pl.pallas_call(
        join_kernel,
        out_shape=(pair,) * chips,
        in_specs=[IN_SMEM, IN_SMEM, IN_VMEM, IN_VMEM],
        out_specs=(IN_VMEM,) * chips,
        compiler_params=KERNEL,
        cost_estimate=SMALL,
    )(chip.reshape(1), core.reshape(1), kept, other)


def body(
    prior_sample,
    measured_point_location,
    measured_data,
    measurement_noise_sigma,
    measured_slots_used,
):
    own_members, cells = prior_sample.shape
    groups = lax.axis_size(MEMBER)
    chips = groups // 2
    total = own_members * groups
    own_cells = cells // groups
    rank = lax.axis_index(MEMBER).astype(jnp.int32)
    chip, core = rank // 2, lax.rem(rank, 2)

    picked = pick(measured_point_location, prior_sample)
    state, picked = lax.optimization_barrier((prior_sample, picked))
    evolved = lax.all_to_all(picked, MEMBER, 0, 0, tiled=True).reshape(total, LANES)

    kept, sent = split(core, state, chips)
    pairs = join(chip, core, kept, swapped(sent))
    evolved, pairs = lax.optimization_barrier((evolved, pairs))

    gram = gram_of(
        rank, measured_slots_used, evolved, measured_data, measurement_noise_sigma
    )
    spaces = lax.axis_size(SPACE)
    first = [shifted(pairs[k], k) for k in FIRST]
    pieces = gram.reshape(spaces, total // spaces, total)
    pieces = jnp.sum(lax.all_to_all(pieces, SPACE, 0, 0, tiled=True), axis=0)
    pieces = jnp.sum(sent_to_all(pieces, MEMBER), axis=0)
    pieces, first, pairs = lax.optimization_barrier((pieces, first, pairs))
    then = [shifted(pairs[k], k) for k in THEN]
    gram = sent_to_all(pieces, SPACE).reshape(total, total)
    transform = transform_of(gram)

    updated = applied(chip, transform, first + then)
    updated = updated.reshape(groups, own_members, own_cells)
    back = lax.all_to_all(updated, MEMBER, 0, 0, tiled=True)
    return back.swapaxes(0, 1).reshape(own_members, cells)


def solution(mesh):
    in_specs = (P(MEMBER, SPACE), P(SPACE, None), P(SPACE, None), P(SPACE, None), P(SPACE))
    return jax.shard_map(
        body, mesh=mesh, in_specs=in_specs, out_specs=P(MEMBER, SPACE), check_vma=False
    )
```

```python
import functools
import math

import jax
import jax.numpy as jnp
from jax import lax
from jax.experimental import pallas as pl
from jax.experimental.pallas import tpu as pltpu
from jax.sharding import PartitionSpec as P

MEMBER = "member"
SPACE = "space"
LANES = 128
SUBLANES = 8
FIRST = (3, 5)
SECOND = (2, 6, 1)
THIRD = (4, 7, 0)
IN_VMEM = pl.BlockSpec(memory_space=pltpu.VMEM)
IN_SMEM = pl.BlockSpec(memory_space=pltpu.SMEM)
KERNEL = pltpu.CompilerParams(vmem_limit_bytes=16 * 2**20)
SMALL = pl.CostEstimate(flops=1024, bytes_accessed=1024, transcendentals=0)


def product(a, b, along):
    return lax.dot_general(
        a,
        b,
        (((1,), (along,)), ((), ())),
        precision=lax.Precision.HIGHEST,
        preferred_element_type=jnp.float32,
    )


def pick_kernel(places_ref, state_ref, out_ref):
    rows, members = out_ref.shape[:2]
    lane = lax.broadcasted_iota(jnp.int32, (members, LANES), 1)

    def one_row(row, carry):
        total = jnp.zeros((members, LANES), jnp.float32)
        for slot in range(LANES):
            place = places_ref[row, slot]
            tile = pl.multiple_of((place >> 7) << 7, LANES)
            cells = state_ref[:, pl.ds(tile, LANES)]
            turned = pltpu.roll(cells, (slot - place) & (LANES - 1), 1)
            total = jnp.where(lane == slot, turned, total)
        out_ref[row] = total
        return carry

    lax.fori_loop(0, rows, one_row, 0)


def pick(places, state):
    return pl.pallas_call(
        pick_kernel,
        out_shape=jax.ShapeDtypeStruct((places.shape[0], state.shape[0], LANES), jnp.float32),
        in_specs=[IN_SMEM, IN_VMEM],
        out_specs=IN_VMEM,
        compiler_params=KERNEL,
        cost_estimate=SMALL,
    )(places, state)


def gram_kernel(rank_ref, used_ref, evolved_ref, data_ref, sigma_ref, out_ref):
    total, obs = evolved_ref.shape
    half = total // 2
    rank = rank_ref[0]
    value = data_ref[pl.ds(rank, 1), :]
    sigma = sigma_ref[pl.ds(rank, 1), :]
    slots = rank * obs + lax.broadcasted_iota(jnp.int32, (1, obs), 1)
    weight = jnp.where(slots < used_ref[0], 1.0 / sigma, 0.0)
    evolved = evolved_ref[...]
    sim_mean = jnp.sum(evolved, axis=0, keepdims=True) * (1.0 / total)
    perturbed = (evolved - sim_mean) * weight
    innovation = jnp.broadcast_to((value - sim_mean) * weight, (SUBLANES, obs))
    out_ref[...] = product(perturbed, perturbed, 1)
    cross = product(innovation, perturbed, 1)
    out_ref[0:1, half:] = cross[0:1, :half]
    out_ref[1:2, half:] = cross[0:1, half:]


def gram_of(rank, used, evolved, data, sigma):
    total = evolved.shape[0]
    return pl.pallas_call(
        gram_kernel,
        out_shape=jax.ShapeDtypeStruct((total, total), jnp.float32),
        in_specs=[IN_SMEM, IN_SMEM, IN_VMEM, IN_VMEM, IN_VMEM],
        out_specs=IN_VMEM,
        compiler_params=KERNEL,
        cost_estimate=SMALL,
    )(rank.reshape(1), used, evolved, data, sigma)


def all_lanes(a, lane):
    return jnp.broadcast_to(a[:, lane : lane + 1], a.shape)


def all_rows(a, row):
    return jnp.broadcast_to(a[row : row + 1, :], a.shape)


def inverse_factor(block):
    size, step = block.shape[0], SUBLANES
    groups = size // step
    row = lax.broadcasted_iota(jnp.int32, (step, size), 0)
    lane = lax.broadcasted_iota(jnp.int32, (step, size), 1)
    left = [block[step * g : step * (g + 1)] for g in range(groups)]
    right = [jnp.where(lane == row + step * g, 1.0, 0.0) for g in range(groups)]
    for p in range(groups):
        left_row = [all_rows(left[p], k) for k in range(step)]
        right_row = [all_rows(right[p], k) for k in range(step)]
        column = [all_lanes(left[p], step * p + j) for j in range(step)]
        a = {(i, j): all_rows(column[j], i) for i in range(step) for j in range(i + 1)}
        factor, scale = {}, []
        for k in range(step):
            scale.append(lax.rsqrt(a[k, k]))
            left_row[k] = left_row[k] * scale[k]
            right_row[k] = right_row[k] * scale[k]
            for i in range(k + 1, step):
                factor[i, k] = a[i, k] * scale[k]
            for i in range(k + 1, step):
                for j in range(k + 1, i + 1):
                    a[i, j] = a[i, j] - factor[i, k] * factor[j, k]
                left_row[i] = left_row[i] - factor[i, k] * left_row[k]
                right_row[i] = right_row[i] - factor[i, k] * right_row[k]
        right[p] = right_row[0]
        for k in range(1, step):
            right[p] = jnp.where(row == k, right_row[k], right[p])
        for g in range(p + 1, groups):
            below = [all_lanes(left[g], step * p + j) for j in range(step)]
            for k in range(step):
                for j in range(k):
                    below[k] = below[k] - below[j] * factor[k, j]
                below[k] = below[k] * scale[k]
            for k in range(step):
                left[g] = left[g] - below[k] * left_row[k]
                right[g] = right[g] - below[k] * right_row[k]
    return jnp.concatenate(right, axis=0)


def transform_kernel(gram_ref, out_ref):
    total = gram_ref.shape[0]
    half = total // 2
    row = lax.broadcasted_iota(jnp.int32, (half, half), 0)
    lane = lax.broadcasted_iota(jnp.int32, (half, half), 1)
    diagonal = jnp.where(row == lane, jnp.float32(total - 1), 0.0)
    first = inverse_factor(gram_ref[:half, :half] + diagonal)
    low = product(gram_ref[half:, :half], first, 1)
    last = inverse_factor(gram_ref[half:, half:] + diagonal - product(low, low, 1))
    corner = -product(last, product(low, first, 0), 0)
    cross_0 = jnp.broadcast_to(gram_ref[0:1, half:], (SUBLANES, half))
    cross_1 = jnp.broadcast_to(gram_ref[1:2, half:], (SUBLANES, half))
    projected_0 = product(cross_0, first, 1)
    projected_1 = product(cross_0, corner, 1) + product(cross_1, last, 1)
    mean_0 = (product(projected_0, first, 0) + product(projected_1, corner, 0))[0:1]
    mean_1 = product(projected_1, last, 0)[0:1]
    spread = math.sqrt(total - 1)
    out_ref[:half, :half] = spread * first + mean_0
    out_ref[:half, half:] = jnp.broadcast_to(mean_1, (half, half))
    out_ref[half:, :half] = spread * corner + mean_0
    out_ref[half:, half:] = spread * last + mean_1


def transform_of(gram):
    return pl.pallas_call(
        transform_kernel,
        out_shape=jax.ShapeDtypeStruct(gram.shape, jnp.float32),
        in_specs=[IN_VMEM],
        out_specs=IN_VMEM,
        compiler_params=KERNEL,
        cost_estimate=SMALL,
    )(gram)


def apply_kernel(chip_ref, transform_ref, *refs):
    *parts, out_ref, state_ref = refs
    chips = len(parts)
    height = parts[0].shape[0]
    for k, part in zip(FIRST + SECOND + THIRD, parts):
        chip = lax.rem(chip_ref[0] - k + chips, chips)
        state_ref[pl.ds(pl.multiple_of(chip * height, height), height), :] = part[...]
    state = state_ref[...]
    average = jnp.sum(state, axis=0, keepdims=True) * (1.0 / state.shape[0])
    out_ref[...] = average + product(transform_ref[...], state - average, 0)


def applied(chip, transform, parts):
    total = transform.shape[0]
    shape = (total, parts[0].shape[1])
    return pl.pallas_call(
        apply_kernel,
        out_shape=jax.ShapeDtypeStruct(shape, jnp.float32),
        in_specs=[IN_SMEM] + [IN_VMEM] * (1 + len(parts)),
        out_specs=IN_VMEM,
        scratch_shapes=[pltpu.VMEM(shape, jnp.float32)],
        compiler_params=pltpu.CompilerParams(vmem_limit_bytes=32 * 2**20),
        cost_estimate=SMALL,
    )(chip.reshape(1), transform, *parts)


def sent_to_all(array, axis):
    size = lax.axis_size(axis)
    copies = jnp.broadcast_to(array[None], (size, *array.shape))
    return lax.all_to_all(copies, axis, 0, 0, tiled=True)


def swapped(array):
    groups = lax.axis_size(MEMBER)
    return lax.ppermute(array, MEMBER, [(i, i ^ 1) for i in range(groups)])


def shifted(array, k):
    if k == 0:
        return array
    groups = lax.axis_size(MEMBER)
    return lax.ppermute(array, MEMBER, [(i, (i + 2 * k) % groups) for i in range(groups)])


def split_kernel(core_ref, state_ref, kept_ref, sent_ref):
    chips, _, width = kept_ref.shape
    core = core_ref[0]
    for chip in range(chips):
        own = pl.multiple_of((2 * chip + core) * width, LANES)
        away = pl.multiple_of((2 * chip + 1 - core) * width, LANES)
        kept_ref[chip] = state_ref[:, pl.ds(own, width)]
        sent_ref[chip] = state_ref[:, pl.ds(away, width)]


def split(core, state, chips):
    members, cells = state.shape
    half = jax.ShapeDtypeStruct((chips, members, cells // chips // 2), jnp.float32)
    return pl.pallas_call(
        split_kernel,
        out_shape=(half, half),
        in_specs=[IN_SMEM, IN_VMEM],
        out_specs=(IN_VMEM, IN_VMEM),
        compiler_params=KERNEL,
        cost_estimate=SMALL,
    )(core.reshape(1), state)


def join_kernel(chip_ref, core_ref, kept_ref, other_ref, *out_refs):
    chips, members, _ = kept_ref.shape
    core = core_ref[0]
    own = pl.ds(pl.multiple_of(core * members, members), members)
    away = pl.ds(pl.multiple_of((1 - core) * members, members), members)
    for k, out_ref in enumerate(out_refs):
        target = lax.rem(chip_ref[0] + k, chips)
        out_ref[own, :] = kept_ref[target]
        out_ref[away, :] = other_ref[target]


def join(chip, core, kept, other):
    chips, members, width = kept.shape
    pair = jax.ShapeDtypeStruct((2 * members, width), jnp.float32)
    return pl.pallas_call(
        join_kernel,
        out_shape=(pair,) * chips,
        in_specs=[IN_SMEM, IN_SMEM, IN_VMEM, IN_VMEM],
        out_specs=(IN_VMEM,) * chips,
        compiler_params=KERNEL,
        cost_estimate=SMALL,
    )(chip.reshape(1), core.reshape(1), kept, other)


def body(
    prior_sample,
    measured_point_location,
    measured_data,
    measurement_noise_sigma,
    measured_slots_used,
):
    own_members, cells = prior_sample.shape
    groups = lax.axis_size(MEMBER)
    chips = groups // 2
    total = own_members * groups
    own_cells = cells // groups
    rank = lax.axis_index(MEMBER).astype(jnp.int32)
    chip, core = rank // 2, lax.rem(rank, 2)

    kept, sent = split(core, prior_sample, chips)
    other = swapped(sent)
    picked = pick(measured_point_location, prior_sample)
    picked, other = lax.optimization_barrier((picked, other))
    evolved = lax.all_to_all(picked, MEMBER, 0, 0, tiled=True).reshape(total, LANES)
    pairs = join(chip, core, kept, other)
    parts = [shifted(pairs[k], k) for k in FIRST]
    evolved, parts, pairs = lax.optimization_barrier((evolved, parts, pairs))

    gram = gram_of(
        rank, measured_slots_used, evolved, measured_data, measurement_noise_sigma
    )
    parts += [shifted(pairs[k], k) for k in SECOND]
    spaces = lax.axis_size(SPACE)
    pieces = gram.reshape(spaces, total // spaces, total)
    pieces = jnp.sum(lax.all_to_all(pieces, SPACE, 0, 0, tiled=True), axis=0)
    pieces = jnp.sum(sent_to_all(pieces, MEMBER), axis=0)
    pieces, parts, pairs = lax.optimization_barrier((pieces, parts, pairs))
    parts += [shifted(pairs[k], k) for k in THIRD]
    gram = sent_to_all(pieces, SPACE).reshape(total, total)
    transform = transform_of(gram)

    updated = applied(chip, transform, parts)
    updated = updated.reshape(groups, own_members, own_cells)
    back = lax.all_to_all(updated, MEMBER, 0, 0, tiled=True)
    return back.swapaxes(0, 1).reshape(own_members, cells)


def solution(mesh):
    in_specs = (P(MEMBER, SPACE), P(SPACE, None), P(SPACE, None), P(SPACE, None), P(SPACE))
    return jax.shard_map(
        body, mesh=mesh, in_specs=in_specs, out_specs=P(MEMBER, SPACE), check_vma=False
    )
```

```python
import functools
import math

import jax
import jax.numpy as jnp
from jax import lax
from jax.experimental import pallas as pl
from jax.experimental.pallas import tpu as pltpu
from jax.sharding import PartitionSpec as P

MEMBER = "member"
SPACE = "space"
LANES = 128
SUBLANES = 8
FIRST = (3, 5, 2)
THEN = (4, 6, 1, 7, 0)
IN_VMEM = pl.BlockSpec(memory_space=pltpu.VMEM)
IN_SMEM = pl.BlockSpec(memory_space=pltpu.SMEM)
KERNEL = pltpu.CompilerParams(vmem_limit_bytes=16 * 2**20)
SMALL = pl.CostEstimate(flops=1024, bytes_accessed=1024, transcendentals=0)


def product(a, b, along):
    return lax.dot_general(
        a,
        b,
        (((1,), (along,)), ((), ())),
        precision=lax.Precision.HIGHEST,
        preferred_element_type=jnp.float32,
    )


def pick_kernel(places_ref, state_ref, out_ref):
    rows, members = out_ref.shape[:2]
    lane = lax.broadcasted_iota(jnp.int32, (members, LANES), 1)

    def one_row(row, carry):
        total = jnp.zeros((members, LANES), jnp.float32)
        for slot in range(LANES):
            place = places_ref[row, slot]
            tile = pl.multiple_of((place >> 7) << 7, LANES)
            cells = state_ref[:, pl.ds(tile, LANES)]
            turned = pltpu.roll(cells, (slot - place) & (LANES - 1), 1)
            total = jnp.where(lane == slot, turned, total)
        out_ref[row] = total
        return carry

    lax.fori_loop(0, rows, one_row, 0)


def pick(places, state):
    return pl.pallas_call(
        pick_kernel,
        out_shape=jax.ShapeDtypeStruct((places.shape[0], state.shape[0], LANES), jnp.float32),
        in_specs=[IN_SMEM, IN_VMEM],
        out_specs=IN_VMEM,
        compiler_params=KERNEL,
        cost_estimate=SMALL,
    )(places, state)


def gram_kernel(rank_ref, used_ref, evolved_ref, data_ref, sigma_ref, out_ref):
    total, obs = evolved_ref.shape
    half = total // 2
    rank = rank_ref[0]
    value = data_ref[pl.ds(rank, 1), :]
    sigma = sigma_ref[pl.ds(rank, 1), :]
    slots = rank * obs + lax.broadcasted_iota(jnp.int32, (1, obs), 1)
    weight = jnp.where(slots < used_ref[0], 1.0 / sigma, 0.0)
    evolved = evolved_ref[...]
    sim_mean = jnp.sum(evolved, axis=0, keepdims=True) * (1.0 / total)
    perturbed = (evolved - sim_mean) * weight
    innovation = jnp.broadcast_to((value - sim_mean) * weight, (SUBLANES, obs))
    out_ref[...] = product(perturbed, perturbed, 1)
    cross = product(innovation, perturbed, 1)
    out_ref[0:1, half:] = cross[0:1, :half]
    out_ref[1:2, half:] = cross[0:1, half:]


def gram_of(rank, used, evolved, data, sigma):
    total = evolved.shape[0]
    return pl.pallas_call(
        gram_kernel,
        out_shape=jax.ShapeDtypeStruct((total, total), jnp.float32),
        in_specs=[IN_SMEM, IN_SMEM, IN_VMEM, IN_VMEM, IN_VMEM],
        out_specs=IN_VMEM,
        compiler_params=KERNEL,
        cost_estimate=SMALL,
    )(rank.reshape(1), used, evolved, data, sigma)


def all_lanes(a, lane):
    return jnp.broadcast_to(a[:, lane : lane + 1], a.shape)


def all_rows(a, row):
    return jnp.broadcast_to(a[row : row + 1, :], a.shape)


def inverse_factor(block):
    size, step = block.shape[0], SUBLANES
    groups = size // step
    row = lax.broadcasted_iota(jnp.int32, (step, size), 0)
    lane = lax.broadcasted_iota(jnp.int32, (step, size), 1)
    left = [block[step * g : step * (g + 1)] for g in range(groups)]
    right = [jnp.where(lane == row + step * g, 1.0, 0.0) for g in range(groups)]
    for p in range(groups):
        left_row = [all_rows(left[p], k) for k in range(step)]
        right_row = [all_rows(right[p], k) for k in range(step)]
        column = [all_lanes(left[p], step * p + j) for j in range(step)]
        a = {(i, j): all_rows(column[j], i) for i in range(step) for j in range(i + 1)}
        factor, scale = {}, []
        for k in range(step):
            scale.append(lax.rsqrt(a[k, k]))
            left_row[k] = left_row[k] * scale[k]
            right_row[k] = right_row[k] * scale[k]
            for i in range(k + 1, step):
                factor[i, k] = a[i, k] * scale[k]
            for i in range(k + 1, step):
                for j in range(k + 1, i + 1):
                    a[i, j] = a[i, j] - factor[i, k] * factor[j, k]
                left_row[i] = left_row[i] - factor[i, k] * left_row[k]
                right_row[i] = right_row[i] - factor[i, k] * right_row[k]
        right[p] = right_row[0]
        for k in range(1, step):
            right[p] = jnp.where(row == k, right_row[k], right[p])
        for g in range(p + 1, groups):
            below = [all_lanes(left[g], step * p + j) for j in range(step)]
            for k in range(step):
                for j in range(k):
                    below[k] = below[k] - below[j] * factor[k, j]
                below[k] = below[k] * scale[k]
            for k in range(step):
                left[g] = left[g] - below[k] * left_row[k]
                right[g] = right[g] - below[k] * right_row[k]
    return jnp.concatenate(right, axis=0)


def transform_kernel(gram_ref, out_ref):
    total = gram_ref.shape[0]
    half = total // 2
    row = lax.broadcasted_iota(jnp.int32, (half, half), 0)
    lane = lax.broadcasted_iota(jnp.int32, (half, half), 1)
    diagonal = jnp.where(row == lane, jnp.float32(total - 1), 0.0)
    first = inverse_factor(gram_ref[:half, :half] + diagonal)
    low = product(gram_ref[half:, :half], first, 1)
    last = inverse_factor(gram_ref[half:, half:] + diagonal - product(low, low, 1))
    corner = -product(last, product(low, first, 0), 0)
    cross_0 = jnp.broadcast_to(gram_ref[0:1, half:], (SUBLANES, half))
    cross_1 = jnp.broadcast_to(gram_ref[1:2, half:], (SUBLANES, half))
    projected_0 = product(cross_0, first, 1)
    projected_1 = product(cross_0, corner, 1) + product(cross_1, last, 1)
    mean_0 = (product(projected_0, first, 0) + product(projected_1, corner, 0))[0:1]
    mean_1 = product(projected_1, last, 0)[0:1]
    spread = math.sqrt(total - 1)
    out_ref[:half, :half] = spread * first + mean_0
    out_ref[:half, half:] = jnp.broadcast_to(mean_1, (half, half))
    out_ref[half:, :half] = spread * corner + mean_0
    out_ref[half:, half:] = spread * last + mean_1


def transform_of(gram):
    return pl.pallas_call(
        transform_kernel,
        out_shape=jax.ShapeDtypeStruct(gram.shape, jnp.float32),
        in_specs=[IN_VMEM],
        out_specs=IN_VMEM,
        compiler_params=KERNEL,
        cost_estimate=SMALL,
    )(gram)


def apply_kernel(chip_ref, transform_ref, *refs):
    *parts, out_ref, state_ref = refs
    chips = len(parts)
    height = parts[0].shape[0]
    for k, part in zip(FIRST + THEN, parts):
        chip = lax.rem(chip_ref[0] - k + chips, chips)
        state_ref[pl.ds(pl.multiple_of(chip * height, height), height), :] = part[...]
    state = state_ref[...]
    average = jnp.sum(state, axis=0, keepdims=True) * (1.0 / state.shape[0])
    out_ref[...] = average + product(transform_ref[...], state - average, 0)


def applied(chip, transform, parts):
    total = transform.shape[0]
    shape = (total, parts[0].shape[1])
    return pl.pallas_call(
        apply_kernel,
        out_shape=jax.ShapeDtypeStruct(shape, jnp.float32),
        in_specs=[IN_SMEM] + [IN_VMEM] * (1 + len(parts)),
        out_specs=IN_VMEM,
        scratch_shapes=[pltpu.VMEM(shape, jnp.float32)],
        compiler_params=pltpu.CompilerParams(vmem_limit_bytes=32 * 2**20),
        cost_estimate=SMALL,
    )(chip.reshape(1), transform, *parts)


def sent_to_all(array, axis):
    size = lax.axis_size(axis)
    copies = jnp.broadcast_to(array[None], (size, *array.shape))
    return lax.all_to_all(copies, axis, 0, 0, tiled=True)


def swapped(array):
    groups = lax.axis_size(MEMBER)
    return lax.ppermute(array, MEMBER, [(i, i ^ 1) for i in range(groups)])


def shifted(array, k):
    if k == 0:
        return array
    groups = lax.axis_size(MEMBER)
    return lax.ppermute(array, MEMBER, [(i, (i + 2 * k) % groups) for i in range(groups)])


def split_kernel(core_ref, state_ref, kept_ref, sent_ref):
    chips, _, width = kept_ref.shape
    core = core_ref[0]
    for chip in range(chips):
        own = pl.multiple_of((2 * chip + core) * width, LANES)
        away = pl.multiple_of((2 * chip + 1 - core) * width, LANES)
        kept_ref[chip] = state_ref[:, pl.ds(own, width)]
        sent_ref[chip] = state_ref[:, pl.ds(away, width)]


def split(core, state, chips):
    members, cells = state.shape
    half = jax.ShapeDtypeStruct((chips, members, cells // chips // 2), jnp.float32)
    return pl.pallas_call(
        split_kernel,
        out_shape=(half, half),
        in_specs=[IN_SMEM, IN_VMEM],
        out_specs=(IN_VMEM, IN_VMEM),
        compiler_params=KERNEL,
        cost_estimate=SMALL,
    )(core.reshape(1), state)


def join_kernel(chip_ref, core_ref, kept_ref, other_ref, *out_refs):
    chips, members, _ = kept_ref.shape
    core = core_ref[0]
    own = pl.ds(pl.multiple_of(core * members, members), members)
    away = pl.ds(pl.multiple_of((1 - core) * members, members), members)
    for k, out_ref in enumerate(out_refs):
        target = lax.rem(chip_ref[0] + k, chips)
        out_ref[own, :] = kept_ref[target]
        out_ref[away, :] = other_ref[target]


def join(chip, core, kept, other):
    chips, members, width = kept.shape
    pair = jax.ShapeDtypeStruct((2 * members, width), jnp.float32)
    return pl.pallas_call(
        join_kernel,
        out_shape=(pair,) * chips,
        in_specs=[IN_SMEM, IN_SMEM, IN_VMEM, IN_VMEM],
        out_specs=(IN_VMEM,) * chips,
        compiler_params=KERNEL,
        cost_estimate=SMALL,
    )(chip.reshape(1), core.reshape(1), kept, other)


def body(
    prior_sample,
    measured_point_location,
    measured_data,
    measurement_noise_sigma,
    measured_slots_used,
):
    own_members, cells = prior_sample.shape
    groups = lax.axis_size(MEMBER)
    chips = groups // 2
    total = own_members * groups
    own_cells = cells // groups
    rank = lax.axis_index(MEMBER).astype(jnp.int32)
    chip, core = rank // 2, lax.rem(rank, 2)

    picked = pick(measured_point_location, prior_sample)
    state, picked = lax.optimization_barrier((prior_sample, picked))
    evolved = lax.all_to_all(picked, MEMBER, 0, 0, tiled=True).reshape(total, LANES)

    kept, sent = split(core, state, chips)
    pairs = join(chip, core, kept, swapped(sent))
    evolved, pairs = lax.optimization_barrier((evolved, pairs))

    gram = gram_of(
        rank, measured_slots_used, evolved, measured_data, measurement_noise_sigma
    )
    spaces = lax.axis_size(SPACE)
    first = [shifted(pairs[k], k) for k in FIRST]
    pieces = gram.reshape(spaces, total // spaces, total)
    pieces = jnp.sum(lax.all_to_all(pieces, SPACE, 0, 0, tiled=True), axis=0)
    pieces = jnp.sum(sent_to_all(pieces, MEMBER), axis=0)
    pieces, first, pairs = lax.optimization_barrier((pieces, first, pairs))
    then = [shifted(pairs[k], k) for k in THEN]
    gram = sent_to_all(pieces, SPACE).reshape(total, total)
    transform = transform_of(gram)

    updated = applied(chip, transform, first + then)
    updated = updated.reshape(groups, own_members, own_cells)
    back = lax.all_to_all(updated, MEMBER, 0, 0, tiled=True)
    return back.swapaxes(0, 1).reshape(own_members, cells)


def solution(mesh):
    in_specs = (P(MEMBER, SPACE), P(SPACE, None), P(SPACE, None), P(SPACE, None), P(SPACE))
    return jax.shard_map(
        body, mesh=mesh, in_specs=in_specs, out_specs=P(MEMBER, SPACE), check_vma=False
    )
```

```python
import functools
import math

import jax
import jax.numpy as jnp
from jax import lax
from jax.experimental import pallas as pl
from jax.experimental.pallas import tpu as pltpu
from jax.sharding import PartitionSpec as P

MEMBER = "member"
SPACE = "space"
LANES = 128
SUBLANES = 8
FIRST = (2, 6, 1)
THEN = (3, 5, 4, 7, 0)
IN_VMEM = pl.BlockSpec(memory_space=pltpu.VMEM)
IN_SMEM = pl.BlockSpec(memory_space=pltpu.SMEM)
KERNEL = pltpu.CompilerParams(vmem_limit_bytes=16 * 2**20)
SMALL = pl.CostEstimate(flops=1024, bytes_accessed=1024, transcendentals=0)


def product(a, b, along):
    return lax.dot_general(
        a,
        b,
        (((1,), (along,)), ((), ())),
        precision=lax.Precision.HIGHEST,
        preferred_element_type=jnp.float32,
    )


def pick_kernel(places_ref, state_ref, out_ref):
    rows, members = out_ref.shape[:2]
    lane = lax.broadcasted_iota(jnp.int32, (members, LANES), 1)

    def one_row(row, carry):
        total = jnp.zeros((members, LANES), jnp.float32)
        for slot in range(LANES):
            place = places_ref[row, slot]
            tile = pl.multiple_of((place >> 7) << 7, LANES)
            cells = state_ref[:, pl.ds(tile, LANES)]
            turned = pltpu.roll(cells, (slot - place) & (LANES - 1), 1)
            total = jnp.where(lane == slot, turned, total)
        out_ref[row] = total
        return carry

    lax.fori_loop(0, rows, one_row, 0)


def pick(places, state):
    return pl.pallas_call(
        pick_kernel,
        out_shape=jax.ShapeDtypeStruct((places.shape[0], state.shape[0], LANES), jnp.float32),
        in_specs=[IN_SMEM, IN_VMEM],
        out_specs=IN_VMEM,
        compiler_params=KERNEL,
        cost_estimate=SMALL,
    )(places, state)


def gram_kernel(rank_ref, used_ref, evolved_ref, data_ref, sigma_ref, out_ref):
    total, obs = evolved_ref.shape
    half = total // 2
    rank = rank_ref[0]
    value = data_ref[pl.ds(rank, 1), :]
    sigma = sigma_ref[pl.ds(rank, 1), :]
    slots = rank * obs + lax.broadcasted_iota(jnp.int32, (1, obs), 1)
    weight = jnp.where(slots < used_ref[0], 1.0 / sigma, 0.0)
    evolved = evolved_ref[...]
    sim_mean = jnp.sum(evolved, axis=0, keepdims=True) * (1.0 / total)
    perturbed = (evolved - sim_mean) * weight
    innovation = jnp.broadcast_to((value - sim_mean) * weight, (SUBLANES, obs))
    out_ref[...] = product(perturbed, perturbed, 1)
    cross = product(innovation, perturbed, 1)
    out_ref[0:1, half:] = cross[0:1, :half]
    out_ref[1:2, half:] = cross[0:1, half:]


def gram_of(rank, used, evolved, data, sigma):
    total = evolved.shape[0]
    return pl.pallas_call(
        gram_kernel,
        out_shape=jax.ShapeDtypeStruct((total, total), jnp.float32),
        in_specs=[IN_SMEM, IN_SMEM, IN_VMEM, IN_VMEM, IN_VMEM],
        out_specs=IN_VMEM,
        compiler_params=KERNEL,
        cost_estimate=SMALL,
    )(rank.reshape(1), used, evolved, data, sigma)


def all_lanes(a, lane):
    return jnp.broadcast_to(a[:, lane : lane + 1], a.shape)


def all_rows(a, row):
    return jnp.broadcast_to(a[row : row + 1, :], a.shape)


def inverse_factor(block):
    size, step = block.shape[0], SUBLANES
    groups = size // step
    row = lax.broadcasted_iota(jnp.int32, (step, size), 0)
    lane = lax.broadcasted_iota(jnp.int32, (step, size), 1)
    left = [block[step * g : step * (g + 1)] for g in range(groups)]
    right = [jnp.where(lane == row + step * g, 1.0, 0.0) for g in range(groups)]
    for p in range(groups):
        left_row = [all_rows(left[p], k) for k in range(step)]
        right_row = [all_rows(right[p], k) for k in range(step)]
        column = [all_lanes(left[p], step * p + j) for j in range(step)]
        a = {(i, j): all_rows(column[j], i) for i in range(step) for j in range(i + 1)}
        factor, scale = {}, []
        for k in range(step):
            scale.append(lax.rsqrt(a[k, k]))
            left_row[k] = left_row[k] * scale[k]
            right_row[k] = right_row[k] * scale[k]
            for i in range(k + 1, step):
                factor[i, k] = a[i, k] * scale[k]
            for i in range(k + 1, step):
                for j in range(k + 1, i + 1):
                    a[i, j] = a[i, j] - factor[i, k] * factor[j, k]
                left_row[i] = left_row[i] - factor[i, k] * left_row[k]
                right_row[i] = right_row[i] - factor[i, k] * right_row[k]
        right[p] = right_row[0]
        for k in range(1, step):
            right[p] = jnp.where(row == k, right_row[k], right[p])
        for g in range(p + 1, groups):
            below = [all_lanes(left[g], step * p + j) for j in range(step)]
            for k in range(step):
                for j in range(k):
                    below[k] = below[k] - below[j] * factor[k, j]
                below[k] = below[k] * scale[k]
            for k in range(step):
                left[g] = left[g] - below[k] * left_row[k]
                right[g] = right[g] - below[k] * right_row[k]
    return jnp.concatenate(right, axis=0)


def transform_kernel(gram_ref, out_ref):
    total = gram_ref.shape[0]
    half = total // 2
    row = lax.broadcasted_iota(jnp.int32, (half, half), 0)
    lane = lax.broadcasted_iota(jnp.int32, (half, half), 1)
    diagonal = jnp.where(row == lane, jnp.float32(total - 1), 0.0)
    first = inverse_factor(gram_ref[:half, :half] + diagonal)
    low = product(gram_ref[half:, :half], first, 1)
    last = inverse_factor(gram_ref[half:, half:] + diagonal - product(low, low, 1))
    corner = -product(last, product(low, first, 0), 0)
    cross_0 = jnp.broadcast_to(gram_ref[0:1, half:], (SUBLANES, half))
    cross_1 = jnp.broadcast_to(gram_ref[1:2, half:], (SUBLANES, half))
    projected_0 = product(cross_0, first, 1)
    projected_1 = product(cross_0, corner, 1) + product(cross_1, last, 1)
    mean_0 = (product(projected_0, first, 0) + product(projected_1, corner, 0))[0:1]
    mean_1 = product(projected_1, last, 0)[0:1]
    spread = math.sqrt(total - 1)
    out_ref[:half, :half] = spread * first + mean_0
    out_ref[:half, half:] = jnp.broadcast_to(mean_1, (half, half))
    out_ref[half:, :half] = spread * corner + mean_0
    out_ref[half:, half:] = spread * last + mean_1


def transform_of(gram):
    return pl.pallas_call(
        transform_kernel,
        out_shape=jax.ShapeDtypeStruct(gram.shape, jnp.float32),
        in_specs=[IN_VMEM],
        out_specs=IN_VMEM,
        compiler_params=KERNEL,
        cost_estimate=SMALL,
    )(gram)


def apply_kernel(chip_ref, transform_ref, *refs):
    *parts, out_ref, state_ref = refs
    chips = len(parts)
    height = parts[0].shape[0]
    for k, part in zip(FIRST + THEN, parts):
        chip = lax.rem(chip_ref[0] - k + chips, chips)
        state_ref[pl.ds(pl.multiple_of(chip * height, height), height), :] = part[...]
    state = state_ref[...]
    average = jnp.sum(state, axis=0, keepdims=True) * (1.0 / state.shape[0])
    out_ref[...] = average + product(transform_ref[...], state - average, 0)


def applied(chip, transform, parts):
    total = transform.shape[0]
    shape = (total, parts[0].shape[1])
    return pl.pallas_call(
        apply_kernel,
        out_shape=jax.ShapeDtypeStruct(shape, jnp.float32),
        in_specs=[IN_SMEM] + [IN_VMEM] * (1 + len(parts)),
        out_specs=IN_VMEM,
        scratch_shapes=[pltpu.VMEM(shape, jnp.float32)],
        compiler_params=pltpu.CompilerParams(vmem_limit_bytes=32 * 2**20),
        cost_estimate=SMALL,
    )(chip.reshape(1), transform, *parts)


def sent_to_all(array, axis):
    size = lax.axis_size(axis)
    copies = jnp.broadcast_to(array[None], (size, *array.shape))
    return lax.all_to_all(copies, axis, 0, 0, tiled=True)


def swapped(array):
    groups = lax.axis_size(MEMBER)
    return lax.ppermute(array, MEMBER, [(i, i ^ 1) for i in range(groups)])


def shifted(array, k):
    if k == 0:
        return array
    groups = lax.axis_size(MEMBER)
    return lax.ppermute(array, MEMBER, [(i, (i + 2 * k) % groups) for i in range(groups)])


def split_kernel(core_ref, state_ref, kept_ref, sent_ref):
    chips, _, width = kept_ref.shape
    core = core_ref[0]
    for chip in range(chips):
        own = pl.multiple_of((2 * chip + core) * width, LANES)
        away = pl.multiple_of((2 * chip + 1 - core) * width, LANES)
        kept_ref[chip] = state_ref[:, pl.ds(own, width)]
        sent_ref[chip] = state_ref[:, pl.ds(away, width)]


def split(core, state, chips):
    members, cells = state.shape
    half = jax.ShapeDtypeStruct((chips, members, cells // chips // 2), jnp.float32)
    return pl.pallas_call(
        split_kernel,
        out_shape=(half, half),
        in_specs=[IN_SMEM, IN_VMEM],
        out_specs=(IN_VMEM, IN_VMEM),
        compiler_params=KERNEL,
        cost_estimate=SMALL,
    )(core.reshape(1), state)


def join_kernel(chip_ref, core_ref, kept_ref, other_ref, *out_refs):
    chips, members, _ = kept_ref.shape
    core = core_ref[0]
    own = pl.ds(pl.multiple_of(core * members, members), members)
    away = pl.ds(pl.multiple_of((1 - core) * members, members), members)
    for k, out_ref in enumerate(out_refs):
        target = lax.rem(chip_ref[0] + k, chips)
        out_ref[own, :] = kept_ref[target]
        out_ref[away, :] = other_ref[target]


def join(chip, core, kept, other):
    chips, members, width = kept.shape
    pair = jax.ShapeDtypeStruct((2 * members, width), jnp.float32)
    return pl.pallas_call(
        join_kernel,
        out_shape=(pair,) * chips,
        in_specs=[IN_SMEM, IN_SMEM, IN_VMEM, IN_VMEM],
        out_specs=(IN_VMEM,) * chips,
        compiler_params=KERNEL,
        cost_estimate=SMALL,
    )(chip.reshape(1), core.reshape(1), kept, other)


def body(
    prior_sample,
    measured_point_location,
    measured_data,
    measurement_noise_sigma,
    measured_slots_used,
):
    own_members, cells = prior_sample.shape
    groups = lax.axis_size(MEMBER)
    chips = groups // 2
    total = own_members * groups
    own_cells = cells // groups
    rank = lax.axis_index(MEMBER).astype(jnp.int32)
    chip, core = rank // 2, lax.rem(rank, 2)

    picked = pick(measured_point_location, prior_sample)
    state, picked = lax.optimization_barrier((prior_sample, picked))
    evolved = lax.all_to_all(picked, MEMBER, 0, 0, tiled=True).reshape(total, LANES)

    kept, sent = split(core, state, chips)
    pairs = join(chip, core, kept, swapped(sent))
    evolved, pairs = lax.optimization_barrier((evolved, pairs))

    gram = gram_of(
        rank, measured_slots_used, evolved, measured_data, measurement_noise_sigma
    )
    spaces = lax.axis_size(SPACE)
    first = [shifted(pairs[k], k) for k in FIRST]
    pieces = gram.reshape(spaces, total // spaces, total)
    pieces = jnp.sum(lax.all_to_all(pieces, SPACE, 0, 0, tiled=True), axis=0)
    pieces = jnp.sum(sent_to_all(pieces, MEMBER), axis=0)
    pieces, first, pairs = lax.optimization_barrier((pieces, first, pairs))
    then = [shifted(pairs[k], k) for k in THEN]
    gram = sent_to_all(pieces, SPACE).reshape(total, total)
    transform = transform_of(gram)

    updated = applied(chip, transform, first + then)
    updated = updated.reshape(groups, own_members, own_cells)
    back = lax.all_to_all(updated, MEMBER, 0, 0, tiled=True)
    return back.swapaxes(0, 1).reshape(own_members, cells)


def solution(mesh):
    in_specs = (P(MEMBER, SPACE), P(SPACE, None), P(SPACE, None), P(SPACE, None), P(SPACE))
    return jax.shard_map(
        body, mesh=mesh, in_specs=in_specs, out_specs=P(MEMBER, SPACE), check_vma=False
    )
```

```python
import functools
import math

import jax
import jax.numpy as jnp
from jax import lax
from jax.experimental import pallas as pl
from jax.experimental.pallas import tpu as pltpu
from jax.sharding import PartitionSpec as P

MEMBER = "member"
SPACE = "space"
LANES = 128
SUBLANES = 8
FIRST = (1, 7)
SECOND = (3, 5)
THIRD = (4, 2, 6, 0)
IN_VMEM = pl.BlockSpec(memory_space=pltpu.VMEM)
IN_SMEM = pl.BlockSpec(memory_space=pltpu.SMEM)
KERNEL = pltpu.CompilerParams(vmem_limit_bytes=16 * 2**20)
SMALL = pl.CostEstimate(flops=1024, bytes_accessed=1024, transcendentals=0)


def product(a, b, along):
    return lax.dot_general(
        a,
        b,
        (((1,), (along,)), ((), ())),
        precision=lax.Precision.HIGHEST,
        preferred_element_type=jnp.float32,
    )


def pick_kernel(places_ref, state_ref, out_ref):
    rows, members = out_ref.shape[:2]
    lane = lax.broadcasted_iota(jnp.int32, (members, LANES), 1)

    def one_row(row, carry):
        total = jnp.zeros((members, LANES), jnp.float32)
        for slot in range(LANES):
            place = places_ref[row, slot]
            tile = pl.multiple_of((place >> 7) << 7, LANES)
            cells = state_ref[:, pl.ds(tile, LANES)]
            turned = pltpu.roll(cells, (slot - place) & (LANES - 1), 1)
            total = jnp.where(lane == slot, turned, total)
        out_ref[row] = total
        return carry

    lax.fori_loop(0, rows, one_row, 0)


def pick(places, state):
    return pl.pallas_call(
        pick_kernel,
        out_shape=jax.ShapeDtypeStruct((places.shape[0], state.shape[0], LANES), jnp.float32),
        in_specs=[IN_SMEM, IN_VMEM],
        out_specs=IN_VMEM,
        compiler_params=KERNEL,
        cost_estimate=SMALL,
    )(places, state)


def gram_kernel(rank_ref, used_ref, evolved_ref, data_ref, sigma_ref, out_ref):
    total, obs = evolved_ref.shape
    half = total // 2
    rank = rank_ref[0]
    value = data_ref[pl.ds(rank, 1), :]
    sigma = sigma_ref[pl.ds(rank, 1), :]
    slots = rank * obs + lax.broadcasted_iota(jnp.int32, (1, obs), 1)
    weight = jnp.where(slots < used_ref[0], 1.0 / sigma, 0.0)
    evolved = evolved_ref[...]
    sim_mean = jnp.sum(evolved, axis=0, keepdims=True) * (1.0 / total)
    perturbed = (evolved - sim_mean) * weight
    innovation = jnp.broadcast_to((value - sim_mean) * weight, (SUBLANES, obs))
    out_ref[...] = product(perturbed, perturbed, 1)
    cross = product(innovation, perturbed, 1)
    out_ref[0:1, half:] = cross[0:1, :half]
    out_ref[1:2, half:] = cross[0:1, half:]


def gram_of(rank, used, evolved, data, sigma):
    total = evolved.shape[0]
    return pl.pallas_call(
        gram_kernel,
        out_shape=jax.ShapeDtypeStruct((total, total), jnp.float32),
        in_specs=[IN_SMEM, IN_SMEM, IN_VMEM, IN_VMEM, IN_VMEM],
        out_specs=IN_VMEM,
        compiler_params=KERNEL,
        cost_estimate=SMALL,
    )(rank.reshape(1), used, evolved, data, sigma)


def all_lanes(a, lane):
    return jnp.broadcast_to(a[:, lane : lane + 1], a.shape)


def all_rows(a, row):
    return jnp.broadcast_to(a[row : row + 1, :], a.shape)


def inverse_factor(block):
    size, step = block.shape[0], SUBLANES
    groups = size // step
    row = lax.broadcasted_iota(jnp.int32, (step, size), 0)
    lane = lax.broadcasted_iota(jnp.int32, (step, size), 1)
    left = [block[step * g : step * (g + 1)] for g in range(groups)]
    right = [jnp.where(lane == row + step * g, 1.0, 0.0) for g in range(groups)]
    for p in range(groups):
        left_row = [all_rows(left[p], k) for k in range(step)]
        right_row = [all_rows(right[p], k) for k in range(step)]
        column = [all_lanes(left[p], step * p + j) for j in range(step)]
        a = {(i, j): all_rows(column[j], i) for i in range(step) for j in range(i + 1)}
        factor, scale = {}, []
        for k in range(step):
            scale.append(lax.rsqrt(a[k, k]))
            left_row[k] = left_row[k] * scale[k]
            right_row[k] = right_row[k] * scale[k]
            for i in range(k + 1, step):
                factor[i, k] = a[i, k] * scale[k]
            for i in range(k + 1, step):
                for j in range(k + 1, i + 1):
                    a[i, j] = a[i, j] - factor[i, k] * factor[j, k]
                left_row[i] = left_row[i] - factor[i, k] * left_row[k]
                right_row[i] = right_row[i] - factor[i, k] * right_row[k]
        right[p] = right_row[0]
        for k in range(1, step):
            right[p] = jnp.where(row == k, right_row[k], right[p])
        for g in range(p + 1, groups):
            below = [all_lanes(left[g], step * p + j) for j in range(step)]
            for k in range(step):
                for j in range(k):
                    below[k] = below[k] - below[j] * factor[k, j]
                below[k] = below[k] * scale[k]
            for k in range(step):
                left[g] = left[g] - below[k] * left_row[k]
                right[g] = right[g] - below[k] * right_row[k]
    return jnp.concatenate(right, axis=0)


def transform_kernel(gram_ref, out_ref):
    total = gram_ref.shape[0]
    half = total // 2
    row = lax.broadcasted_iota(jnp.int32, (half, half), 0)
    lane = lax.broadcasted_iota(jnp.int32, (half, half), 1)
    diagonal = jnp.where(row == lane, jnp.float32(total - 1), 0.0)
    first = inverse_factor(gram_ref[:half, :half] + diagonal)
    low = product(gram_ref[half:, :half], first, 1)
    last = inverse_factor(gram_ref[half:, half:] + diagonal - product(low, low, 1))
    corner = -product(last, product(low, first, 0), 0)
    cross_0 = jnp.broadcast_to(gram_ref[0:1, half:], (SUBLANES, half))
    cross_1 = jnp.broadcast_to(gram_ref[1:2, half:], (SUBLANES, half))
    projected_0 = product(cross_0, first, 1)
    projected_1 = product(cross_0, corner, 1) + product(cross_1, last, 1)
    mean_0 = (product(projected_0, first, 0) + product(projected_1, corner, 0))[0:1]
    mean_1 = product(projected_1, last, 0)[0:1]
    spread = math.sqrt(total - 1)
    out_ref[:half, :half] = spread * first + mean_0
    out_ref[:half, half:] = jnp.broadcast_to(mean_1, (half, half))
    out_ref[half:, :half] = spread * corner + mean_0
    out_ref[half:, half:] = spread * last + mean_1


def transform_of(gram):
    return pl.pallas_call(
        transform_kernel,
        out_shape=jax.ShapeDtypeStruct(gram.shape, jnp.float32),
        in_specs=[IN_VMEM],
        out_specs=IN_VMEM,
        compiler_params=KERNEL,
        cost_estimate=SMALL,
    )(gram)


def apply_kernel(chip_ref, transform_ref, *refs):
    *parts, out_ref, state_ref = refs
    chips = len(parts)
    height = parts[0].shape[0]
    for k, part in zip(FIRST + SECOND + THIRD, parts):
        chip = lax.rem(chip_ref[0] - k + chips, chips)
        state_ref[pl.ds(pl.multiple_of(chip * height, height), height), :] = part[...]
    state = state_ref[...]
    average = jnp.sum(state, axis=0, keepdims=True) * (1.0 / state.shape[0])
    out_ref[...] = average + product(transform_ref[...], state - average, 0)


def applied(chip, transform, parts):
    total = transform.shape[0]
    shape = (total, parts[0].shape[1])
    return pl.pallas_call(
        apply_kernel,
        out_shape=jax.ShapeDtypeStruct(shape, jnp.float32),
        in_specs=[IN_SMEM] + [IN_VMEM] * (1 + len(parts)),
        out_specs=IN_VMEM,
        scratch_shapes=[pltpu.VMEM(shape, jnp.float32)],
        compiler_params=pltpu.CompilerParams(vmem_limit_bytes=32 * 2**20),
        cost_estimate=SMALL,
    )(chip.reshape(1), transform, *parts)


def sent_to_all(array, axis):
    size = lax.axis_size(axis)
    copies = jnp.broadcast_to(array[None], (size, *array.shape))
    return lax.all_to_all(copies, axis, 0, 0, tiled=True)


def swapped(array):
    groups = lax.axis_size(MEMBER)
    return lax.ppermute(array, MEMBER, [(i, i ^ 1) for i in range(groups)])


def shifted(array, k):
    if k == 0:
        return array
    groups = lax.axis_size(MEMBER)
    return lax.ppermute(array, MEMBER, [(i, (i + 2 * k) % groups) for i in range(groups)])


def split_kernel(core_ref, state_ref, kept_ref, sent_ref):
    chips, _, width = kept_ref.shape
    core = core_ref[0]
    for chip in range(chips):
        own = pl.multiple_of((2 * chip + core) * width, LANES)
        away = pl.multiple_of((2 * chip + 1 - core) * width, LANES)
        kept_ref[chip] = state_ref[:, pl.ds(own, width)]
        sent_ref[chip] = state_ref[:, pl.ds(away, width)]


def split(core, state, chips):
    members, cells = state.shape
    half = jax.ShapeDtypeStruct((chips, members, cells // chips // 2), jnp.float32)
    return pl.pallas_call(
        split_kernel,
        out_shape=(half, half),
        in_specs=[IN_SMEM, IN_VMEM],
        out_specs=(IN_VMEM, IN_VMEM),
        compiler_params=KERNEL,
        cost_estimate=SMALL,
    )(core.reshape(1), state)


def join_kernel(chip_ref, core_ref, kept_ref, other_ref, *out_refs):
    chips, members, _ = kept_ref.shape
    core = core_ref[0]
    own = pl.ds(pl.multiple_of(core * members, members), members)
    away = pl.ds(pl.multiple_of((1 - core) * members, members), members)
    for k, out_ref in enumerate(out_refs):
        target = lax.rem(chip_ref[0] + k, chips)
        out_ref[own, :] = kept_ref[target]
        out_ref[away, :] = other_ref[target]


def join(chip, core, kept, other):
    chips, members, width = kept.shape
    pair = jax.ShapeDtypeStruct((2 * members, width), jnp.float32)
    return pl.pallas_call(
        join_kernel,
        out_shape=(pair,) * chips,
        in_specs=[IN_SMEM, IN_SMEM, IN_VMEM, IN_VMEM],
        out_specs=(IN_VMEM,) * chips,
        compiler_params=KERNEL,
        cost_estimate=SMALL,
    )(chip.reshape(1), core.reshape(1), kept, other)


def body(
    prior_sample,
    measured_point_location,
    measured_data,
    measurement_noise_sigma,
    measured_slots_used,
):
    own_members, cells = prior_sample.shape
    groups = lax.axis_size(MEMBER)
    chips = groups // 2
    total = own_members * groups
    own_cells = cells // groups
    rank = lax.axis_index(MEMBER).astype(jnp.int32)
    chip, core = rank // 2, lax.rem(rank, 2)

    picked = pick(measured_point_location, prior_sample)
    state, picked = lax.optimization_barrier((prior_sample, picked))
    evolved = lax.all_to_all(picked, MEMBER, 0, 0, tiled=True).reshape(total, LANES)

    kept, sent = split(core, state, chips)
    pairs = join(chip, core, kept, swapped(sent))
    evolved, pairs = lax.optimization_barrier((evolved, pairs))

    gram = gram_of(
        rank, measured_slots_used, evolved, measured_data, measurement_noise_sigma
    )
    parts = [shifted(pairs[k], k) for k in FIRST]
    pieces = gram.reshape(groups, own_members, total)
    pieces = jnp.sum(lax.all_to_all(pieces, MEMBER, 0, 0, tiled=True), axis=0)
    pieces, parts, pairs = lax.optimization_barrier((pieces, parts, pairs))
    parts += [shifted(pairs[k], k) for k in SECOND]
    pieces = jnp.sum(sent_to_all(pieces, SPACE), axis=0)
    pieces, parts, pairs = lax.optimization_barrier((pieces, parts, pairs))
    parts += [shifted(pairs[k], k) for k in THIRD]
    gram = sent_to_all(pieces, MEMBER).reshape(total, total)
    transform = transform_of(gram)

    updated = applied(chip, transform, parts)
    updated = updated.reshape(groups, own_members, own_cells)
    back = lax.all_to_all(updated, MEMBER, 0, 0, tiled=True)
    return back.swapaxes(0, 1).reshape(own_members, cells)


def solution(mesh):
    in_specs = (P(MEMBER, SPACE), P(SPACE, None), P(SPACE, None), P(SPACE, None), P(SPACE))
    return jax.shard_map(
        body, mesh=mesh, in_specs=in_specs, out_specs=P(MEMBER, SPACE), check_vma=False
    )
```

```python
import functools
import math

import jax
import jax.numpy as jnp
from jax import lax
from jax.experimental import pallas as pl
from jax.experimental.pallas import tpu as pltpu
from jax.sharding import PartitionSpec as P

MEMBER = "member"
SPACE = "space"
LANES = 128
SUBLANES = 8
SOON = (1,7)
FIRST = (3, 5, 2, 6)
THEN = (4, 0)
IN_VMEM = pl.BlockSpec(memory_space=pltpu.VMEM)
IN_SMEM = pl.BlockSpec(memory_space=pltpu.SMEM)
KERNEL = pltpu.CompilerParams(vmem_limit_bytes=16 * 2**20)
LARGE = pl.CostEstimate(flops=2**34, bytes_accessed=2**26, transcendentals=0)
SMALL = pl.CostEstimate(flops=1024, bytes_accessed=1024, transcendentals=0)


def product(a, b, along):
    return lax.dot_general(
        a,
        b,
        (((1,), (along,)), ((), ())),
        precision=lax.Precision.HIGHEST,
        preferred_element_type=jnp.float32,
    )


def pick_kernel(places_ref, state_ref, out_ref):
    rows, members = out_ref.shape[:2]
    lane = lax.broadcasted_iota(jnp.int32, (members, LANES), 1)

    def one_row(row, carry):
        total = jnp.zeros((members, LANES), jnp.float32)
        for slot in range(LANES):
            place = places_ref[row, slot]
            tile = pl.multiple_of((place >> 7) << 7, LANES)
            cells = state_ref[:, pl.ds(tile, LANES)]
            turned = pltpu.roll(cells, (slot - place) & (LANES - 1), 1)
            total = jnp.where(lane == slot, turned, total)
        out_ref[row] = total
        return carry

    lax.fori_loop(0, rows, one_row, 0)


def pick(places, state):
    return pl.pallas_call(
        pick_kernel,
        out_shape=jax.ShapeDtypeStruct((places.shape[0], state.shape[0], LANES), jnp.float32),
        in_specs=[IN_SMEM, IN_VMEM],
        out_specs=IN_VMEM,
        compiler_params=KERNEL,
        cost_estimate=SMALL,
    )(places, state)


def gram_kernel(rank_ref, used_ref, evolved_ref, data_ref, sigma_ref, out_ref):
    total, obs = evolved_ref.shape
    half = total // 2
    rank = rank_ref[0]
    value = data_ref[pl.ds(rank, 1), :]
    sigma = sigma_ref[pl.ds(rank, 1), :]
    slots = rank * obs + lax.broadcasted_iota(jnp.int32, (1, obs), 1)
    weight = jnp.where(slots < used_ref[0], 1.0 / sigma, 0.0)
    evolved = evolved_ref[...]
    sim_mean = jnp.sum(evolved, axis=0, keepdims=True) * (1.0 / total)
    perturbed = (evolved - sim_mean) * weight
    innovation = jnp.broadcast_to((value - sim_mean) * weight, (SUBLANES, obs))
    out_ref[...] = product(perturbed, perturbed, 1)
    cross = product(innovation, perturbed, 1)
    out_ref[0:1, half:] = cross[0:1, :half]
    out_ref[1:2, half:] = cross[0:1, half:]


def gram_of(rank, used, evolved, data, sigma):
    total = evolved.shape[0]
    return pl.pallas_call(
        gram_kernel,
        out_shape=jax.ShapeDtypeStruct((total, total), jnp.float32),
        in_specs=[IN_SMEM, IN_SMEM, IN_VMEM, IN_VMEM, IN_VMEM],
        out_specs=IN_VMEM,
        compiler_params=KERNEL,
        cost_estimate=LARGE,
    )(rank.reshape(1), used, evolved, data, sigma)


def all_lanes(a, lane):
    return jnp.broadcast_to(a[:, lane : lane + 1], a.shape)


def all_rows(a, row):
    return jnp.broadcast_to(a[row : row + 1, :], a.shape)


def inverse_factor(block):
    size, step = block.shape[0], SUBLANES
    groups = size // step
    row = lax.broadcasted_iota(jnp.int32, (step, size), 0)
    lane = lax.broadcasted_iota(jnp.int32, (step, size), 1)
    left = [block[step * g : step * (g + 1)] for g in range(groups)]
    right = [jnp.where(lane == row + step * g, 1.0, 0.0) for g in range(groups)]
    for p in range(groups):
        left_row = [all_rows(left[p], k) for k in range(step)]
        right_row = [all_rows(right[p], k) for k in range(step)]
        column = [all_lanes(left[p], step * p + j) for j in range(step)]
        a = {(i, j): all_rows(column[j], i) for i in range(step) for j in range(i + 1)}
        factor, scale = {}, []
        for k in range(step):
            scale.append(lax.rsqrt(a[k, k]))
            left_row[k] = left_row[k] * scale[k]
            right_row[k] = right_row[k] * scale[k]
            for i in range(k + 1, step):
                factor[i, k] = a[i, k] * scale[k]
            for i in range(k + 1, step):
                for j in range(k + 1, i + 1):
                    a[i, j] = a[i, j] - factor[i, k] * factor[j, k]
                left_row[i] = left_row[i] - factor[i, k] * left_row[k]
                right_row[i] = right_row[i] - factor[i, k] * right_row[k]
        right[p] = right_row[0]
        for k in range(1, step):
            right[p] = jnp.where(row == k, right_row[k], right[p])
        for g in range(p + 1, groups):
            below = [all_lanes(left[g], step * p + j) for j in range(step)]
            for k in range(step):
                for j in range(k):
                    below[k] = below[k] - below[j] * factor[k, j]
                below[k] = below[k] * scale[k]
            for k in range(step):
                left[g] = left[g] - below[k] * left_row[k]
                right[g] = right[g] - below[k] * right_row[k]
    return jnp.concatenate(right, axis=0)


def transform_kernel(gram_ref, out_ref):
    total = gram_ref.shape[0]
    half = total // 2
    row = lax.broadcasted_iota(jnp.int32, (half, half), 0)
    lane = lax.broadcasted_iota(jnp.int32, (half, half), 1)
    diagonal = jnp.where(row == lane, jnp.float32(total - 1), 0.0)
    first = inverse_factor(gram_ref[:half, :half] + diagonal)
    low = product(gram_ref[half:, :half], first, 1)
    last = inverse_factor(gram_ref[half:, half:] + diagonal - product(low, low, 1))
    corner = -product(last, product(low, first, 0), 0)
    cross_0 = jnp.broadcast_to(gram_ref[0:1, half:], (SUBLANES, half))
    cross_1 = jnp.broadcast_to(gram_ref[1:2, half:], (SUBLANES, half))
    projected_0 = product(cross_0, first, 1)
    projected_1 = product(cross_0, corner, 1) + product(cross_1, last, 1)
    mean_0 = (product(projected_0, first, 0) + product(projected_1, corner, 0))[0:1]
    mean_1 = product(projected_1, last, 0)[0:1]
    spread = math.sqrt(total - 1)
    out_ref[:half, :half] = spread * first + mean_0
    out_ref[:half, half:] = jnp.broadcast_to(mean_1, (half, half))
    out_ref[half:, :half] = spread * corner + mean_0
    out_ref[half:, half:] = spread * last + mean_1


def transform_of(gram):
    return pl.pallas_call(
        transform_kernel,
        out_shape=jax.ShapeDtypeStruct(gram.shape, jnp.float32),
        in_specs=[IN_VMEM],
        out_specs=IN_VMEM,
        compiler_params=KERNEL,
        cost_estimate=SMALL,
    )(gram)


def apply_kernel(chip_ref, transform_ref, *refs):
    *parts, out_ref, state_ref = refs
    chips = len(parts)
    height = parts[0].shape[0]
    for k, part in zip(SOON + FIRST + THEN, parts):
        chip = lax.rem(chip_ref[0] - k + chips, chips)
        state_ref[pl.ds(pl.multiple_of(chip * height, height), height), :] = part[...]
    state = state_ref[...]
    average = jnp.sum(state, axis=0, keepdims=True) * (1.0 / state.shape[0])
    out_ref[...] = average + product(transform_ref[...], state - average, 0)


def applied(chip, transform, parts):
    total = transform.shape[0]
    shape = (total, parts[0].shape[1])
    return pl.pallas_call(
        apply_kernel,
        out_shape=jax.ShapeDtypeStruct(shape, jnp.float32),
        in_specs=[IN_SMEM] + [IN_VMEM] * (1 + len(parts)),
        out_specs=IN_VMEM,
        scratch_shapes=[pltpu.VMEM(shape, jnp.float32)],
        compiler_params=pltpu.CompilerParams(vmem_limit_bytes=32 * 2**20),
        cost_estimate=SMALL,
    )(chip.reshape(1), transform, *parts)


def sent_to_all(array, axis):
    size = lax.axis_size(axis)
    copies = jnp.broadcast_to(array[None], (size, *array.shape))
    return lax.all_to_all(copies, axis, 0, 0, tiled=True)


def swapped(array):
    groups = lax.axis_size(MEMBER)
    return lax.ppermute(array, MEMBER, [(i, i ^ 1) for i in range(groups)])


def shifted(array, k):
    if k == 0:
        return array
    groups = lax.axis_size(MEMBER)
    return lax.ppermute(array, MEMBER, [(i, (i + 2 * k) % groups) for i in range(groups)])


def split_kernel(core_ref, state_ref, kept_ref, sent_ref):
    chips, _, width = kept_ref.shape
    core = core_ref[0]
    for chip in range(chips):
        own = pl.multiple_of((2 * chip + core) * width, LANES)
        away = pl.multiple_of((2 * chip + 1 - core) * width, LANES)
        kept_ref[chip] = state_ref[:, pl.ds(own, width)]
        sent_ref[chip] = state_ref[:, pl.ds(away, width)]


def split(core, state, chips):
    members, cells = state.shape
    half = jax.ShapeDtypeStruct((chips, members, cells // chips // 2), jnp.float32)
    return pl.pallas_call(
        split_kernel,
        out_shape=(half, half),
        in_specs=[IN_SMEM, IN_VMEM],
        out_specs=(IN_VMEM, IN_VMEM),
        compiler_params=KERNEL,
        cost_estimate=SMALL,
    )(core.reshape(1), state)


def join_kernel(chip_ref, core_ref, kept_ref, other_ref, *out_refs):
    chips, members, _ = kept_ref.shape
    core = core_ref[0]
    own = pl.ds(pl.multiple_of(core * members, members), members)
    away = pl.ds(pl.multiple_of((1 - core) * members, members), members)
    for k, out_ref in enumerate(out_refs):
        target = lax.rem(chip_ref[0] + k, chips)
        out_ref[own, :] = kept_ref[target]
        out_ref[away, :] = other_ref[target]


def join(chip, core, kept, other):
    chips, members, width = kept.shape
    pair = jax.ShapeDtypeStruct((2 * members, width), jnp.float32)
    return pl.pallas_call(
        join_kernel,
        out_shape=(pair,) * chips,
        in_specs=[IN_SMEM, IN_SMEM, IN_VMEM, IN_VMEM],
        out_specs=(IN_VMEM,) * chips,
        compiler_params=KERNEL,
        cost_estimate=SMALL,
    )(chip.reshape(1), core.reshape(1), kept, other)


def body(
    prior_sample,
    measured_point_location,
    measured_data,
    measurement_noise_sigma,
    measured_slots_used,
):
    own_members, cells = prior_sample.shape
    groups = lax.axis_size(MEMBER)
    chips = groups // 2
    total = own_members * groups
    own_cells = cells // groups
    rank = lax.axis_index(MEMBER).astype(jnp.int32)
    chip, core = rank // 2, lax.rem(rank, 2)

    picked = pick(measured_point_location, prior_sample)
    state, picked = lax.optimization_barrier((prior_sample, picked))
    evolved = lax.all_to_all(picked, MEMBER, 0, 0, tiled=True).reshape(total, LANES)

    kept, sent = split(core, state, chips)
    pairs = join(chip, core, kept, swapped(sent))
    soon = [shifted(pairs[k], k) for k in SOON]
    evolved, pairs = lax.optimization_barrier((evolved, pairs))

    gram = gram_of(
        rank, measured_slots_used, evolved, measured_data, measurement_noise_sigma
    )
    spaces = lax.axis_size(SPACE)
    gram, soon = lax.optimization_barrier((gram, soon))
    first = [shifted(pairs[k], k) for k in FIRST]
    pieces = gram.reshape(spaces, total // spaces, total)
    pieces = jnp.sum(lax.all_to_all(pieces, SPACE, 0, 0, tiled=True), axis=0)
    pieces = jnp.sum(sent_to_all(pieces, MEMBER), axis=0)
    pieces, first, pairs = lax.optimization_barrier((pieces, first, pairs))
    then = [shifted(pairs[k], k) for k in THEN]
    gram = sent_to_all(pieces, SPACE).reshape(total, total)
    transform = transform_of(gram)

    updated = applied(chip, transform, soon + first + then)
    updated = updated.reshape(groups, own_members, own_cells)
    back = lax.all_to_all(updated, MEMBER, 0, 0, tiled=True)
    return back.swapaxes(0, 1).reshape(own_members, cells)


def solution(mesh):
    in_specs = (P(MEMBER, SPACE), P(SPACE, None), P(SPACE, None), P(SPACE, None), P(SPACE))
    return jax.shard_map(
        body, mesh=mesh, in_specs=in_specs, out_specs=P(MEMBER, SPACE), check_vma=False
    )
```

```python
import functools
import math

import jax
import jax.numpy as jnp
from jax import lax
from jax.experimental import pallas as pl
from jax.experimental.pallas import tpu as pltpu
from jax.sharding import PartitionSpec as P

MEMBER = "member"
SPACE = "space"
LANES = 128
SUBLANES = 8
FIRST = (3, 5, 2, 6)
THEN = (4, 1, 7, 0)
IN_VMEM = pl.BlockSpec(memory_space=pltpu.VMEM)
IN_SMEM = pl.BlockSpec(memory_space=pltpu.SMEM)
KERNEL = pltpu.CompilerParams(vmem_limit_bytes=16 * 2**20)
LARGE = pl.CostEstimate(flops=2**34, bytes_accessed=2**26, transcendentals=0)
SMALL = pl.CostEstimate(flops=1024, bytes_accessed=1024, transcendentals=0)


def product(a, b, along):
    return lax.dot_general(
        a,
        b,
        (((1,), (along,)), ((), ())),
        precision=lax.Precision.HIGHEST,
        preferred_element_type=jnp.float32,
    )


def pick_kernel(places_ref, lanes_ref, state_ref, out_ref):
    rows, members = out_ref.shape[:2]
    lane = lax.broadcasted_iota(jnp.int32, (members, LANES), 1)

    def one_row(row, carry):
        within = lanes_ref[pl.ds(row, 1), :] & (LANES - 1)
        within = jnp.broadcast_to(within, (members, LANES))
        total = jnp.zeros((members, LANES), jnp.float32)
        for slot in range(LANES):
            tile = pl.multiple_of((places_ref[row, slot] >> 7) << 7, LANES)
            cells = state_ref[:, pl.ds(tile, LANES)]
            found = jnp.take_along_axis(cells, within, axis=1)
            total = jnp.where(lane == slot, found, total)
        out_ref[row] = total
        return carry

    lax.fori_loop(0, rows, one_row, 0)


def pick(places, state):
    return pl.pallas_call(
        pick_kernel,
        out_shape=jax.ShapeDtypeStruct((places.shape[0], state.shape[0], LANES), jnp.float32),
        in_specs=[IN_SMEM, IN_VMEM, IN_VMEM],
        out_specs=IN_VMEM,
        compiler_params=KERNEL,
        cost_estimate=SMALL,
    )(places, places, state)


def gram_kernel(rank_ref, used_ref, evolved_ref, data_ref, sigma_ref, out_ref):
    total, obs = evolved_ref.shape
    half = total // 2
    rank = rank_ref[0]
    value = data_ref[pl.ds(rank, 1), :]
    sigma = sigma_ref[pl.ds(rank, 1), :]
    slots = rank * obs + lax.broadcasted_iota(jnp.int32, (1, obs), 1)
    weight = jnp.where(slots < used_ref[0], 1.0 / sigma, 0.0)
    evolved = evolved_ref[...]
    sim_mean = jnp.sum(evolved, axis=0, keepdims=True) * (1.0 / total)
    perturbed = (evolved - sim_mean) * weight
    innovation = jnp.broadcast_to((value - sim_mean) * weight, (SUBLANES, obs))
    out_ref[...] = product(perturbed, perturbed, 1)
    cross = product(innovation, perturbed, 1)
    out_ref[0:1, half:] = cross[0:1, :half]
    out_ref[1:2, half:] = cross[0:1, half:]


def gram_of(rank, used, evolved, data, sigma):
    total = evolved.shape[0]
    return pl.pallas_call(
        gram_kernel,
        out_shape=jax.ShapeDtypeStruct((total, total), jnp.float32),
        in_specs=[IN_SMEM, IN_SMEM, IN_VMEM, IN_VMEM, IN_VMEM],
        out_specs=IN_VMEM,
        compiler_params=KERNEL,
        cost_estimate=LARGE,
    )(rank.reshape(1), used, evolved, data, sigma)


def all_lanes(a, lane):
    return jnp.broadcast_to(a[:, lane : lane + 1], a.shape)


def all_rows(a, row):
    return jnp.broadcast_to(a[row : row + 1, :], a.shape)


def inverse_factor(block):
    size, step = block.shape[0], SUBLANES
    groups = size // step
    row = lax.broadcasted_iota(jnp.int32, (step, size), 0)
    lane = lax.broadcasted_iota(jnp.int32, (step, size), 1)
    left = [block[step * g : step * (g + 1)] for g in range(groups)]
    right = [jnp.where(lane == row + step * g, 1.0, 0.0) for g in range(groups)]
    for p in range(groups):
        left_row = [all_rows(left[p], k) for k in range(step)]
        right_row = [all_rows(right[p], k) for k in range(step)]
        column = [all_lanes(left[p], step * p + j) for j in range(step)]
        a = {(i, j): all_rows(column[j], i) for i in range(step) for j in range(i + 1)}
        factor, scale = {}, []
        for k in range(step):
            scale.append(lax.rsqrt(a[k, k]))
            left_row[k] = left_row[k] * scale[k]
            right_row[k] = right_row[k] * scale[k]
            for i in range(k + 1, step):
                factor[i, k] = a[i, k] * scale[k]
            for i in range(k + 1, step):
                for j in range(k + 1, i + 1):
                    a[i, j] = a[i, j] - factor[i, k] * factor[j, k]
                left_row[i] = left_row[i] - factor[i, k] * left_row[k]
                right_row[i] = right_row[i] - factor[i, k] * right_row[k]
        right[p] = right_row[0]
        for k in range(1, step):
            right[p] = jnp.where(row == k, right_row[k], right[p])
        for g in range(p + 1, groups):
            below = [all_lanes(left[g], step * p + j) for j in range(step)]
            for k in range(step):
                for j in range(k):
                    below[k] = below[k] - below[j] * factor[k, j]
                below[k] = below[k] * scale[k]
            for k in range(step):
                left[g] = left[g] - below[k] * left_row[k]
                right[g] = right[g] - below[k] * right_row[k]
    return jnp.concatenate(right, axis=0)


def transform_kernel(gram_ref, out_ref):
    total = gram_ref.shape[0]
    half = total // 2
    row = lax.broadcasted_iota(jnp.int32, (half, half), 0)
    lane = lax.broadcasted_iota(jnp.int32, (half, half), 1)
    diagonal = jnp.where(row == lane, jnp.float32(total - 1), 0.0)
    first = inverse_factor(gram_ref[:half, :half] + diagonal)
    low = product(gram_ref[half:, :half], first, 1)
    last = inverse_factor(gram_ref[half:, half:] + diagonal - product(low, low, 1))
    corner = -product(last, product(low, first, 0), 0)
    cross_0 = jnp.broadcast_to(gram_ref[0:1, half:], (SUBLANES, half))
    cross_1 = jnp.broadcast_to(gram_ref[1:2, half:], (SUBLANES, half))
    projected_0 = product(cross_0, first, 1)
    projected_1 = product(cross_0, corner, 1) + product(cross_1, last, 1)
    mean_0 = (product(projected_0, first, 0) + product(projected_1, corner, 0))[0:1]
    mean_1 = product(projected_1, last, 0)[0:1]
    spread = math.sqrt(total - 1)
    out_ref[:half, :half] = spread * first + mean_0
    out_ref[:half, half:] = jnp.broadcast_to(mean_1, (half, half))
    out_ref[half:, :half] = spread * corner + mean_0
    out_ref[half:, half:] = spread * last + mean_1


def transform_of(gram):
    return pl.pallas_call(
        transform_kernel,
        out_shape=jax.ShapeDtypeStruct(gram.shape, jnp.float32),
        in_specs=[IN_VMEM],
        out_specs=IN_VMEM,
        compiler_params=KERNEL,
        cost_estimate=SMALL,
    )(gram)


def apply_kernel(chip_ref, transform_ref, *refs):
    *parts, out_ref, state_ref = refs
    chips = len(parts)
    height = parts[0].shape[0]
    for k, part in zip(FIRST + THEN, parts):
        chip = lax.rem(chip_ref[0] - k + chips, chips)
        state_ref[pl.ds(pl.multiple_of(chip * height, height), height), :] = part[...]
    state = state_ref[...]
    average = jnp.sum(state, axis=0, keepdims=True) * (1.0 / state.shape[0])
    out_ref[...] = average + product(transform_ref[...], state - average, 0)


def applied(chip, transform, parts):
    total = transform.shape[0]
    shape = (total, parts[0].shape[1])
    return pl.pallas_call(
        apply_kernel,
        out_shape=jax.ShapeDtypeStruct(shape, jnp.float32),
        in_specs=[IN_SMEM] + [IN_VMEM] * (1 + len(parts)),
        out_specs=IN_VMEM,
        scratch_shapes=[pltpu.VMEM(shape, jnp.float32)],
        compiler_params=pltpu.CompilerParams(vmem_limit_bytes=32 * 2**20),
        cost_estimate=SMALL,
    )(chip.reshape(1), transform, *parts)


def spread_kernel(parts_ref, out_ref):
    total = parts_ref[0]
    for part in range(1, parts_ref.shape[0]):
        total = total + parts_ref[part]
    for copy in range(out_ref.shape[0]):
        out_ref[copy] = total


def sum_sent_to_all(parts, axis):
    copies = pl.pallas_call(
        spread_kernel,
        out_shape=jax.ShapeDtypeStruct((lax.axis_size(axis), *parts.shape[1:]), jnp.float32),
        in_specs=[IN_VMEM],
        out_specs=IN_VMEM,
        compiler_params=KERNEL,
        cost_estimate=SMALL,
    )(parts)
    return lax.all_to_all(copies, axis, 0, 0, tiled=True)


def swapped(array):
    groups = lax.axis_size(MEMBER)
    return lax.ppermute(array, MEMBER, [(i, i ^ 1) for i in range(groups)])


def shifted(array, k):
    if k == 0:
        return array
    groups = lax.axis_size(MEMBER)
    return lax.ppermute(array, MEMBER, [(i, (i + 2 * k) % groups) for i in range(groups)])


def split_kernel(core_ref, state_ref, kept_ref, sent_ref):
    chips, _, width = kept_ref.shape
    core = core_ref[0]
    for chip in range(chips):
        own = pl.multiple_of((2 * chip + core) * width, LANES)
        away = pl.multiple_of((2 * chip + 1 - core) * width, LANES)
        kept_ref[chip] = state_ref[:, pl.ds(own, width)]
        sent_ref[chip] = state_ref[:, pl.ds(away, width)]


def split(core, state, chips):
    members, cells = state.shape
    half = jax.ShapeDtypeStruct((chips, members, cells // chips // 2), jnp.float32)
    return pl.pallas_call(
        split_kernel,
        out_shape=(half, half),
        in_specs=[IN_SMEM, IN_VMEM],
        out_specs=(IN_VMEM, IN_VMEM),
        compiler_params=KERNEL,
        cost_estimate=SMALL,
    )(core.reshape(1), state)


def join_kernel(chip_ref, core_ref, kept_ref, other_ref, *out_refs):
    chips, members, _ = kept_ref.shape
    core = core_ref[0]
    own = pl.ds(pl.multiple_of(core * members, members), members)
    away = pl.ds(pl.multiple_of((1 - core) * members, members), members)
    for k, out_ref in enumerate(out_refs):
        target = lax.rem(chip_ref[0] + k, chips)
        out_ref[own, :] = kept_ref[target]
        out_ref[away, :] = other_ref[target]


def join(chip, core, kept, other):
    chips, members, width = kept.shape
    pair = jax.ShapeDtypeStruct((2 * members, width), jnp.float32)
    return pl.pallas_call(
        join_kernel,
        out_shape=(pair,) * chips,
        in_specs=[IN_SMEM, IN_SMEM, IN_VMEM, IN_VMEM],
        out_specs=(IN_VMEM,) * chips,
        compiler_params=KERNEL,
        cost_estimate=SMALL,
    )(chip.reshape(1), core.reshape(1), kept, other)


def body(
    prior_sample,
    measured_point_location,
    measured_data,
    measurement_noise_sigma,
    measured_slots_used,
):
    own_members, cells = prior_sample.shape
    groups = lax.axis_size(MEMBER)
    chips = groups // 2
    total = own_members * groups
    own_cells = cells // groups
    rank = lax.axis_index(MEMBER).astype(jnp.int32)
    chip, core = rank // 2, lax.rem(rank, 2)

    picked = pick(measured_point_location, prior_sample)
    state, picked = lax.optimization_barrier((prior_sample, picked))
    evolved = lax.all_to_all(picked, MEMBER, 0, 0, tiled=True).reshape(total, LANES)

    kept, sent = split(core, state, chips)
    pairs = join(chip, core, kept, swapped(sent))

    gram = gram_of(
        rank, measured_slots_used, evolved, measured_data, measurement_noise_sigma
    )
    spaces = lax.axis_size(SPACE)
    first = [shifted(pairs[k], k) for k in FIRST]
    pieces = gram.reshape(spaces, total // spaces, total)
    pieces = lax.all_to_all(pieces, SPACE, 0, 0, tiled=True)
    pieces = sum_sent_to_all(pieces, MEMBER)
    pieces, first, pairs = lax.optimization_barrier((pieces, first, pairs))
    then = [shifted(pairs[k], k) for k in THEN]
    gram = sum_sent_to_all(pieces, SPACE).reshape(total, total)
    transform = transform_of(gram)

    updated = applied(chip, transform, first + then)
    updated = updated.reshape(groups, own_members, own_cells)
    back = lax.all_to_all(updated, MEMBER, 0, 0, tiled=True)
    return back.swapaxes(0, 1).reshape(own_members, cells)


def solution(mesh):
    in_specs = (P(MEMBER, SPACE), P(SPACE, None), P(SPACE, None), P(SPACE, None), P(SPACE))
    return jax.shard_map(
        body, mesh=mesh, in_specs=in_specs, out_specs=P(MEMBER, SPACE), check_vma=False
    )
```

```python
import functools
import math

import jax
import jax.numpy as jnp
from jax import lax
from jax.experimental import pallas as pl
from jax.experimental.pallas import tpu as pltpu
from jax.sharding import PartitionSpec as P

MEMBER = "member"
SPACE = "space"
LANES = 128
SUBLANES = 8
FIRST = (2, 6, 1, 7)
THEN = (3, 5, 4, 0)
IN_VMEM = pl.BlockSpec(memory_space=pltpu.VMEM)
IN_SMEM = pl.BlockSpec(memory_space=pltpu.SMEM)
KERNEL = pltpu.CompilerParams(vmem_limit_bytes=16 * 2**20)
LARGE = pl.CostEstimate(flops=2**34, bytes_accessed=2**26, transcendentals=0)
SMALL = pl.CostEstimate(flops=1024, bytes_accessed=1024, transcendentals=0)


def product(a, b, along):
    return lax.dot_general(
        a,
        b,
        (((1,), (along,)), ((), ())),
        precision=lax.Precision.HIGHEST,
        preferred_element_type=jnp.float32,
    )


def pick_kernel(places_ref, lanes_ref, state_ref, out_ref):
    rows, members = out_ref.shape[:2]
    lane = lax.broadcasted_iota(jnp.int32, (members, LANES), 1)

    def one_row(row, carry):
        within = lanes_ref[pl.ds(row, 1), :] & (LANES - 1)
        within = jnp.broadcast_to(within, (members, LANES))
        total = jnp.zeros((members, LANES), jnp.float32)
        for slot in range(LANES):
            tile = pl.multiple_of((places_ref[row, slot] >> 7) << 7, LANES)
            cells = state_ref[:, pl.ds(tile, LANES)]
            found = jnp.take_along_axis(cells, within, axis=1)
            total = jnp.where(lane == slot, found, total)
        out_ref[row] = total
        return carry

    lax.fori_loop(0, rows, one_row, 0)


def pick(places, state):
    return pl.pallas_call(
        pick_kernel,
        out_shape=jax.ShapeDtypeStruct((places.shape[0], state.shape[0], LANES), jnp.float32),
        in_specs=[IN_SMEM, IN_VMEM, IN_VMEM],
        out_specs=IN_VMEM,
        compiler_params=KERNEL,
        cost_estimate=SMALL,
    )(places, places, state)


def gram_kernel(rank_ref, used_ref, evolved_ref, data_ref, sigma_ref, out_ref):
    total, obs = evolved_ref.shape
    half = total // 2
    rank = rank_ref[0]
    value = data_ref[pl.ds(rank, 1), :]
    sigma = sigma_ref[pl.ds(rank, 1), :]
    slots = rank * obs + lax.broadcasted_iota(jnp.int32, (1, obs), 1)
    weight = jnp.where(slots < used_ref[0], 1.0 / sigma, 0.0)
    evolved = evolved_ref[...]
    sim_mean = jnp.sum(evolved, axis=0, keepdims=True) * (1.0 / total)
    perturbed = (evolved - sim_mean) * weight
    innovation = jnp.broadcast_to((value - sim_mean) * weight, (SUBLANES, obs))
    out_ref[...] = product(perturbed, perturbed, 1)
    cross = product(innovation, perturbed, 1)
    out_ref[0:1, half:] = cross[0:1, :half]
    out_ref[1:2, half:] = cross[0:1, half:]


def gram_of(rank, used, evolved, data, sigma):
    total = evolved.shape[0]
    return pl.pallas_call(
        gram_kernel,
        out_shape=jax.ShapeDtypeStruct((total, total), jnp.float32),
        in_specs=[IN_SMEM, IN_SMEM, IN_VMEM, IN_VMEM, IN_VMEM],
        out_specs=IN_VMEM,
        compiler_params=KERNEL,
        cost_estimate=LARGE,
    )(rank.reshape(1), used, evolved, data, sigma)


def all_lanes(a, lane):
    return jnp.broadcast_to(a[:, lane : lane + 1], a.shape)


def all_rows(a, row):
    return jnp.broadcast_to(a[row : row + 1, :], a.shape)


def inverse_factor(block):
    size, step = block.shape[0], SUBLANES
    groups = size // step
    row = lax.broadcasted_iota(jnp.int32, (step, size), 0)
    lane = lax.broadcasted_iota(jnp.int32, (step, size), 1)
    left = [block[step * g : step * (g + 1)] for g in range(groups)]
    right = [jnp.where(lane == row + step * g, 1.0, 0.0) for g in range(groups)]
    for p in range(groups):
        left_row = [all_rows(left[p], k) for k in range(step)]
        right_row = [all_rows(right[p], k) for k in range(step)]
        column = [all_lanes(left[p], step * p + j) for j in range(step)]
        a = {(i, j): all_rows(column[j], i) for i in range(step) for j in range(i + 1)}
        factor, scale = {}, []
        for k in range(step):
            scale.append(lax.rsqrt(a[k, k]))
            left_row[k] = left_row[k] * scale[k]
            right_row[k] = right_row[k] * scale[k]
            for i in range(k + 1, step):
                factor[i, k] = a[i, k] * scale[k]
            for i in range(k + 1, step):
                for j in range(k + 1, i + 1):
                    a[i, j] = a[i, j] - factor[i, k] * factor[j, k]
                left_row[i] = left_row[i] - factor[i, k] * left_row[k]
                right_row[i] = right_row[i] - factor[i, k] * right_row[k]
        right[p] = right_row[0]
        for k in range(1, step):
            right[p] = jnp.where(row == k, right_row[k], right[p])
        for g in range(p + 1, groups):
            below = [all_lanes(left[g], step * p + j) for j in range(step)]
            for k in range(step):
                for j in range(k):
                    below[k] = below[k] - below[j] * factor[k, j]
                below[k] = below[k] * scale[k]
            for k in range(step):
                left[g] = left[g] - below[k] * left_row[k]
                right[g] = right[g] - below[k] * right_row[k]
    return jnp.concatenate(right, axis=0)


def transform_kernel(gram_ref, out_ref):
    total = gram_ref.shape[0]
    half = total // 2
    row = lax.broadcasted_iota(jnp.int32, (half, half), 0)
    lane = lax.broadcasted_iota(jnp.int32, (half, half), 1)
    diagonal = jnp.where(row == lane, jnp.float32(total - 1), 0.0)
    first = inverse_factor(gram_ref[:half, :half] + diagonal)
    low = product(gram_ref[half:, :half], first, 1)
    last = inverse_factor(gram_ref[half:, half:] + diagonal - product(low, low, 1))
    corner = -product(last, product(low, first, 0), 0)
    cross_0 = jnp.broadcast_to(gram_ref[0:1, half:], (SUBLANES, half))
    cross_1 = jnp.broadcast_to(gram_ref[1:2, half:], (SUBLANES, half))
    projected_0 = product(cross_0, first, 1)
    projected_1 = product(cross_0, corner, 1) + product(cross_1, last, 1)
    mean_0 = (product(projected_0, first, 0) + product(projected_1, corner, 0))[0:1]
    mean_1 = product(projected_1, last, 0)[0:1]
    spread = math.sqrt(total - 1)
    out_ref[:half, :half] = spread * first + mean_0
    out_ref[:half, half:] = jnp.broadcast_to(mean_1, (half, half))
    out_ref[half:, :half] = spread * corner + mean_0
    out_ref[half:, half:] = spread * last + mean_1


def transform_of(gram):
    return pl.pallas_call(
        transform_kernel,
        out_shape=jax.ShapeDtypeStruct(gram.shape, jnp.float32),
        in_specs=[IN_VMEM],
        out_specs=IN_VMEM,
        compiler_params=KERNEL,
        cost_estimate=SMALL,
    )(gram)


def apply_kernel(chip_ref, transform_ref, *refs):
    *parts, out_ref, state_ref = refs
    chips = len(parts)
    height = parts[0].shape[0]
    for k, part in zip(FIRST + THEN, parts):
        chip = lax.rem(chip_ref[0] - k + chips, chips)
        state_ref[pl.ds(pl.multiple_of(chip * height, height), height), :] = part[...]
    state = state_ref[...]
    average = jnp.sum(state, axis=0, keepdims=True) * (1.0 / state.shape[0])
    out_ref[...] = average + product(transform_ref[...], state - average, 0)


def applied(chip, transform, parts):
    total = transform.shape[0]
    shape = (total, parts[0].shape[1])
    return pl.pallas_call(
        apply_kernel,
        out_shape=jax.ShapeDtypeStruct(shape, jnp.float32),
        in_specs=[IN_SMEM] + [IN_VMEM] * (1 + len(parts)),
        out_specs=IN_VMEM,
        scratch_shapes=[pltpu.VMEM(shape, jnp.float32)],
        compiler_params=pltpu.CompilerParams(vmem_limit_bytes=32 * 2**20),
        cost_estimate=SMALL,
    )(chip.reshape(1), transform, *parts)


def spread_kernel(parts_ref, out_ref):
    total = parts_ref[0]
    for part in range(1, parts_ref.shape[0]):
        total = total + parts_ref[part]
    for copy in range(out_ref.shape[0]):
        out_ref[copy] = total


def sum_sent_to_all(parts, axis):
    copies = pl.pallas_call(
        spread_kernel,
        out_shape=jax.ShapeDtypeStruct((lax.axis_size(axis), *parts.shape[1:]), jnp.float32),
        in_specs=[IN_VMEM],
        out_specs=IN_VMEM,
        compiler_params=KERNEL,
        cost_estimate=SMALL,
    )(parts)
    return lax.all_to_all(copies, axis, 0, 0, tiled=True)


def swapped(array):
    groups = lax.axis_size(MEMBER)
    return lax.ppermute(array, MEMBER, [(i, i ^ 1) for i in range(groups)])


def shifted(array, k):
    if k == 0:
        return array
    groups = lax.axis_size(MEMBER)
    return lax.ppermute(array, MEMBER, [(i, (i + 2 * k) % groups) for i in range(groups)])


def split_kernel(core_ref, state_ref, kept_ref, sent_ref):
    chips, _, width = kept_ref.shape
    core = core_ref[0]
    for chip in range(chips):
        own = pl.multiple_of((2 * chip + core) * width, LANES)
        away = pl.multiple_of((2 * chip + 1 - core) * width, LANES)
        kept_ref[chip] = state_ref[:, pl.ds(own, width)]
        sent_ref[chip] = state_ref[:, pl.ds(away, width)]


def split(core, state, chips):
    members, cells = state.shape
    half = jax.ShapeDtypeStruct((chips, members, cells // chips // 2), jnp.float32)
    return pl.pallas_call(
        split_kernel,
        out_shape=(half, half),
        in_specs=[IN_SMEM, IN_VMEM],
        out_specs=(IN_VMEM, IN_VMEM),
        compiler_params=KERNEL,
        cost_estimate=SMALL,
    )(core.reshape(1), state)


def join_kernel(chip_ref, core_ref, kept_ref, other_ref, *out_refs):
    chips, members, _ = kept_ref.shape
    core = core_ref[0]
    own = pl.ds(pl.multiple_of(core * members, members), members)
    away = pl.ds(pl.multiple_of((1 - core) * members, members), members)
    for k, out_ref in enumerate(out_refs):
        target = lax.rem(chip_ref[0] + k, chips)
        out_ref[own, :] = kept_ref[target]
        out_ref[away, :] = other_ref[target]


def join(chip, core, kept, other):
    chips, members, width = kept.shape
    pair = jax.ShapeDtypeStruct((2 * members, width), jnp.float32)
    return pl.pallas_call(
        join_kernel,
        out_shape=(pair,) * chips,
        in_specs=[IN_SMEM, IN_SMEM, IN_VMEM, IN_VMEM],
        out_specs=(IN_VMEM,) * chips,
        compiler_params=KERNEL,
        cost_estimate=SMALL,
    )(chip.reshape(1), core.reshape(1), kept, other)


def body(
    prior_sample,
    measured_point_location,
    measured_data,
    measurement_noise_sigma,
    measured_slots_used,
):
    own_members, cells = prior_sample.shape
    groups = lax.axis_size(MEMBER)
    chips = groups // 2
    total = own_members * groups
    own_cells = cells // groups
    rank = lax.axis_index(MEMBER).astype(jnp.int32)
    chip, core = rank // 2, lax.rem(rank, 2)

    picked = pick(measured_point_location, prior_sample)
    state, picked = lax.optimization_barrier((prior_sample, picked))
    evolved = lax.all_to_all(picked, MEMBER, 0, 0, tiled=True).reshape(total, LANES)

    kept, sent = split(core, state, chips)
    pairs = join(chip, core, kept, swapped(sent))

    gram = gram_of(
        rank, measured_slots_used, evolved, measured_data, measurement_noise_sigma
    )
    spaces = lax.axis_size(SPACE)
    first = [shifted(pairs[k], k) for k in FIRST]
    pieces = gram.reshape(spaces, total // spaces, total)
    pieces = lax.all_to_all(pieces, SPACE, 0, 0, tiled=True)
    pieces = sum_sent_to_all(pieces, MEMBER)
    pieces, first, pairs = lax.optimization_barrier((pieces, first, pairs))
    then = [shifted(pairs[k], k) for k in THEN]
    gram = sum_sent_to_all(pieces, SPACE).reshape(total, total)
    transform = transform_of(gram)

    updated = applied(chip, transform, first + then)
    updated = updated.reshape(groups, own_members, own_cells)
    back = lax.all_to_all(updated, MEMBER, 0, 0, tiled=True)
    return back.swapaxes(0, 1).reshape(own_members, cells)


def solution(mesh):
    in_specs = (P(MEMBER, SPACE), P(SPACE, None), P(SPACE, None), P(SPACE, None), P(SPACE))
    return jax.shard_map(
        body, mesh=mesh, in_specs=in_specs, out_specs=P(MEMBER, SPACE), check_vma=False
    )
```
